256 devices in a mesh: gx: 64 (over z, x, core), gz: 4 (over y).
Axes of the slice: x: 4, y: 4, z: 8, core: 2. Of those that a mesh axis runs over, the one named last changes fastest.
Arguments:
- fields: float32 [3, 4096, 12288], P(None, 'gx', 'gz'), may hold values from -6 to 6
- register: float32 [3, 4096, 12288], P(None, 'gx', 'gz'), may hold values from -3 to 3
- source: float32 [4096, 12288], P('gx', 'gz'), may hold values from -0.25 to 0.25
- metric: float32 [4096], P('gx'), may hold values from 0.5 to 2
- curvature: float32 [4096], P('gx'), may hold values from -12 to 12
Outputs:
- new_fields: float32 [3, 4096, 12288], P(None, 'gx', 'gz')
- new_register: float32 [3, 4096, 12288], P(None, 'gx', 'gz')
- velocity: float32 [4096, 12288], P('gx', 'gz')
The draws below stay inside these ranges and needn't reach their ends.
All inputs are finite; a program needn't handle non-finite values. Where the reference program divides by a largest or mean magnitude, that divisor is 1e-20 or more.
Results may differ from the reference program's by a relative error of at most 0.0001.
Values sent between devices are 32-bit elements; how exact they have to be, the bound alone decides.
No kernel may reach another device: no remote copies, remote signals or barrier semaphores. Data moves between devices by JAX's collectives and lax.ppermute only.
A program may use at most 64 MiB of HBM per device.

```python
import jax
import jax.numpy as jnp
from jax import lax

NX = 4096
NL = 12288


def shard_levels(own_key, extent, pieces, smallest, largest):
    factor_of, own = 1.0, jax.random.fold_in(own_key, 6)
    for dim, parts in pieces:
        draws = jnp.exp(jax.random.uniform(jax.random.fold_in(own, dim), (parts,), jnp.float32, smallest / len(pieces), largest / len(pieces)))
        factor_of = factor_of * jnp.repeat(draws, extent[dim] // parts).reshape([-1 if axis == dim else 1 for axis in range(len(extent))])
    return factor_of


def gaussian(stream_key, extent, deviation, limit, shards=(), held_as=jnp.bfloat16):
    drawn = jax.random.normal(stream_key, extent, jnp.float32) * deviation
    if len(shards) > 0:
        drawn = shard_levels(stream_key, extent, shards, -0.22, 0.18) * drawn
    return jnp.clip(drawn, min=-limit, max=limit).astype(held_as)


def setup_inputs(seed: int = 0) -> dict:
    streams_of = jax.random.split(jax.random.key(seed), 6)
    fields = gaussian(streams_of[0], (3, NX, NL), 1.0, 6.0, ((1, 64), (2, 4)), jnp.float32)
    register = gaussian(streams_of[1], (3, NX, NL), 0.5, 3.0, ((1, 64), (2, 4)), jnp.float32)
    source = gaussian(streams_of[2], (NX, NL), 0.03125, 0.25, ((0, 64), (1, 4)), jnp.float32)
    metric = jnp.clip(0.5 + 1.5 * jax.random.uniform(streams_of[3], (NX,), jnp.float32) ** shard_levels(streams_of[3], (NX,), ((0, 64),), -0.2, 0.2), 0.5, 2.0)
    curvature = gaussian(streams_of[4], (NX,), 3.0, 12.0, ((0, 64),), jnp.float32)
    return {"fields": fields, "register": register, "source": source, "metric": metric, "curvature": curvature}


ALPHA_ONE = 1.0 / 3.0
COEF_ONE = 14.0 / 9.0
WIDE_ONE = 1.0 / 9.0
ALPHA_TWO = 2.0 / 11.0
COEF_TWO = 12.0 / 11.0
WIDE_TWO = 3.0 / 11.0
VISCOSITY = 0.25
DIFFUSIVITY = 0.2
COURANT = 1.2
KEEP_FACTOR = -5.0 / 9.0
STEP_FACTOR = 15.0 / 16.0

def pad_cells(values):
    return jnp.pad(values, ((2, 2), (0, 0)))

def first_right(padded):
    return COEF_ONE / 2.0 * (padded[3:-1] - padded[1:-3]) + WIDE_ONE / 4.0 * (padded[4:] - padded[:-4])

def second_right(padded):
    centre = padded[2:-2]
    near = padded[3:-1] - 2.0 * centre + padded[1:-3]
    far = padded[4:] - 2.0 * centre + padded[:-4]
    return COEF_TWO * near + WIDE_TWO / 4.0 * far

def solve_lines(alpha, right_side):
    length = right_side.shape[0]
    offdiag = jnp.full((length,), alpha, jnp.float32)
    below_diag = offdiag.at[0].set(0.0)
    above_diag = offdiag.at[length - 1].set(0.0)
    diagonal = jnp.ones((length,), jnp.float32)
    return lax.linalg.tridiagonal_solve(below_diag, diagonal, above_diag, right_side)

def reference(fields, register, source, metric, curvature):
    stretch = metric[:, None]
    curving = curvature[:, None]
    scaled_source = source / stretch
    velocity = -(jnp.cumsum(scaled_source, axis=0) - 0.5 * scaled_source)
    max_rate = jnp.max(jnp.abs(velocity) * stretch + 4.0 * VISCOSITY * stretch * stretch)
    time_step = COURANT / max_rate
    velocity_x = stretch * solve_lines(ALPHA_ONE, first_right(pad_cells(velocity)))
    field_list = []
    register_list = []
    for component in range(3):
        field = fields[component]
        padded = pad_cells(field)
        slope = solve_lines(ALPHA_ONE, first_right(padded))
        bend = solve_lines(ALPHA_TWO, second_right(padded))
        field_x = stretch * slope
        field_xx = stretch * stretch * bend + curving * slope
        diffusion = VISCOSITY if component < 2 else DIFFUSIVITY
        tendency = -(velocity * field_x + field * velocity_x) + diffusion * field_xx
        updated = KEEP_FACTOR * register[component] + time_step * tendency
        register_list.append(updated)
        field_list.append(field + STEP_FACTOR * updated)
    return (jnp.stack(field_list), jnp.stack(register_list), velocity)
```

```python
import functools

import jax
import jax.numpy as jnp
import numpy as np
from jax import lax
from jax.experimental import pallas as pl
from jax.experimental.pallas import tpu as pltpu
from jax.sharding import Mesh
from jax.sharding import PartitionSpec as P

ALPHA_ONE = 1.0 / 3.0
COEF_ONE = 14.0 / 9.0
WIDE_ONE = 1.0 / 9.0
ALPHA_TWO = 2.0 / 11.0
COEF_TWO = 12.0 / 11.0
WIDE_TWO = 3.0 / 11.0
VISCOSITY = 0.25
DIFFUSIVITY = 0.2
COURANT = 1.2
KEEP_FACTOR = -5.0 / 9.0
STEP_FACTOR = 15.0 / 16.0

LANES = 128
CHUNK = 1024
MESSAGE = 16
DEPTH = 256


def inverse(alpha, length):
    matrix = np.eye(length) + alpha * (np.eye(length, k=1) + np.eye(length, k=-1))
    return np.linalg.inv(matrix)


@functools.cache
def operators(cells):
    length = 4 * cells
    near_up, near_down = np.eye(length, k=1), np.eye(length, k=-1)
    far_up, far_down = np.eye(length, k=2), np.eye(length, k=-2)
    first = COEF_ONE / 2.0 * (near_up - near_down) + WIDE_ONE / 4.0 * (far_up - far_down)
    second = COEF_TWO * (near_up - 2.0 * np.eye(length) + near_down) + WIDE_TWO / 4.0 * (
        far_up - 2.0 * np.eye(length) + far_down
    )
    slope = inverse(ALPHA_ONE, length) @ first
    bend = inverse(ALPHA_TWO, length) @ second
    integral = -(np.tril(np.ones((length, length))) - 0.5 * np.eye(length))
    constant = slope @ np.ones(length)
    return slope, bend, slope @ integral, constant


def from_left(matrix, block, cells):
    start = block * cells
    part = matrix[start : start + cells, start - cells : start]
    weights = part[1]
    factors = part[:, cells - 2] / part[1, cells - 2]
    corner = np.zeros(cells)
    corner[0] = part[0, cells - 1] - factors[0] * part[1, cells - 1]
    return factors, weights, corner


def from_right(matrix, block, cells):
    start = block * cells
    part = matrix[start : start + cells, start + cells : start + 2 * cells]
    weights = part[cells - 2]
    factors = part[:, 1] / part[cells - 2, 1]
    corner = np.zeros(cells)
    corner[cells - 1] = part[cells - 1, 0] - factors[cells - 1] * part[cells - 2, 0]
    return factors, weights, corner


@functools.cache
def tables(cells):
    slope, bend, drift, constant = operators(cells)
    kinds = (0, 2, 1, 3)
    send = np.zeros((4, cells, LANES))
    solve = np.zeros((4, 3, cells, DEPTH))
    for kind, block in enumerate(kinds):
        odd = kind >= 2
        start = block * cells
        own = slice(start, start + cells)
        rest = np.zeros(4 * cells)
        if block == 3:
            rest[own] = constant[own]
        local = drift + rest[:, None] * (np.arange(4 * cells) < start)[None, :]
        for which, matrix in enumerate((slope, bend, local)):
            base = np.zeros((cells, cells + 8))
            base[:, :cells] = matrix[own, own]
            left, right = (0, 4) if odd else (4, 0)
            slot = 1 if which == 1 else 0
            if block > 0:
                factors, _, corner = from_left(matrix, block, cells)
                base[:, cells + left + slot] = factors
                base[:, cells + left + 2] = corner
            if block < 3:
                factors, _, corner = from_right(matrix, block, cells)
                base[:, cells + right + slot] = factors
                base[:, cells + right + 2] = corner
            if which == 2:
                base[:, cells + 1] = -rest[own]
            for copy in range(3):
                solve[kind, which, :, copy * cells : (copy + 1) * cells] = base[:, :cells]
                solve[kind, which, :, 3 * cells + 8 * copy : 3 * cells + 8 * copy + 8] = base[:, cells:]
            to_right = to_left = np.zeros(cells)
            sent = (slope, bend, drift)[which]
            if block < 2:
                to_right = from_left(sent, block + 1, cells)[1]
            elif block == 2:
                to_right = from_left(sent, 2, cells)[1]
            if block > 0:
                to_left = from_right(sent, block - 1, cells)[1]
            pair = (to_left, to_right) if odd else (to_right, to_left)
            send[kind, :, which] = pair[0]
            send[kind, :, 3 + which] = pair[1]
    return send.astype(np.float32), solve.astype(np.float32)


def column(row):
    size = row.shape[1]
    rows = lax.broadcasted_iota(jnp.int32, (size, size), 0)
    columns = lax.broadcasted_iota(jnp.int32, (size, size), 1)
    spread = jnp.broadcast_to(row, (size, size))
    return jnp.sum(jnp.where(rows == columns, spread, 0.0), axis=1, keepdims=True)


def halves(value):
    high = value.astype(jnp.bfloat16)
    low = (value - high.astype(jnp.float32)).astype(jnp.bfloat16)
    return high, low


def send_kernel(where, fields, source, metric, weights, totals, message_one, message_two):
    cells = source.shape[0]
    odd = where[0] >= 2
    scaled = source[...] * (1.0 / column(metric[...]))
    total = jnp.sum(scaled, axis=0, keepdims=True)
    for peer in range(totals.shape[0]):
        for k in range(CHUNK // LANES):
            totals[peer, k : k + 1, :] = total[:, k * LANES : (k + 1) * LANES]
    blank = jnp.zeros((1, CHUNK), jnp.float32)
    for k in range(4):
        value = fields[k] if k < 3 else scaled
        first, last = value[:1], value[cells - 1 :]
        for message, begin in ((message_one, 0), (message_two, 3)):
            row = 4 * k
            if k < 3:
                for which in range(2):
                    weight = weights[0, :, begin + which : begin + which + 1]
                    message[row + which : row + which + 1, :] = jnp.sum(value * weight, axis=0, keepdims=True)
            else:
                weight = weights[0, :, begin + 2 : begin + 3]
                message[row : row + 1, :] = jnp.sum(value * weight, axis=0, keepdims=True)
                message[row + 1 : row + 2, :] = blank
            edge = jnp.where(odd, first, last) if begin == 0 else jnp.where(odd, last, first)
            message[row + 2 : row + 3, :] = edge
            message[row + 3 : row + 4, :] = blank


def velocity_kernel(place, source, metric, inner, outer, lower, velocity, offset, rate, peak):
    step = pl.program_id(0)
    stretch = column(metric[...])
    scaled = source[...] * (1.0 / stretch)
    high = scaled.astype(jnp.bfloat16)
    rest = scaled - high.astype(jnp.float32)
    middle = rest.astype(jnp.bfloat16)
    low = (rest - middle.astype(jnp.float32)).astype(jnp.bfloat16)
    pieces = jnp.concatenate([high, middle, low], axis=0)
    running = jnp.dot(lower[...], pieces, preferred_element_type=jnp.float32)
    before = jnp.zeros((CHUNK // LANES, LANES), jnp.float32)
    for peer in range(inner.shape[0]):
        before += jnp.where(peer < place[0], inner[peer], 0.0)
    for peer in range(outer.shape[0]):
        before += jnp.where(peer < place[1], outer[peer], 0.0)
    shift = jnp.concatenate([before[k : k + 1, :] for k in range(CHUNK // LANES)], axis=1)
    offset[...] = shift
    value = -(running + shift)
    velocity[...] = value
    here = jnp.abs(value) * stretch + 4.0 * VISCOSITY * stretch * stretch
    top = jnp.max(jnp.max(here, axis=0, keepdims=True), axis=1, keepdims=True)

    @pl.when(step == 0)
    def _():
        peak[...] = jnp.broadcast_to(top, peak.shape)

    @pl.when(step > 0)
    def _():
        peak[...] = jnp.maximum(peak[...], top)

    @pl.when(step == pl.num_programs(0) - 1)
    def _():
        rate[...] = jnp.broadcast_to(peak[:1, :], rate.shape)


def update_kernel(
    where, fields, register, source, velocity, offset, message_one, message_two, metric, curvature, rates, table,
    new_fields, new_register, mixed, mixed_scalar, drift,
):
    cells = source.shape[0]
    stretch = column(metric[...])

    @pl.when(pl.program_id(0) == 0)
    def _():
        curving = column(curvature[...])
        slope, bend = table[0, 0], table[0, 1]
        lane = lax.broadcasted_iota(jnp.int32, (cells, DEPTH), 1)
        is_low = ((lane >= 2 * cells) & (lane < 3 * cells)) | (lane >= 3 * cells + 16)

        def split(value):
            high, low = halves(value)
            return jnp.where(is_low, low.astype(jnp.float32), high.astype(jnp.float32)).astype(jnp.bfloat16)

        field_x = stretch * slope
        field_xx = stretch * stretch * bend + curving * slope
        mixed[:cells, :] = split(field_x)
        mixed[cells:, :] = split(VISCOSITY * field_xx)
        mixed_scalar[:cells, :] = mixed[:cells, :]
        mixed_scalar[cells:, :] = split(DIFFUSIVITY * field_xx)
        drift[...] = split(stretch * table[0, 2])

    def stacked(value, tail):
        high, low = halves(value)
        tail_high = tail.astype(jnp.bfloat16).astype(jnp.float32)
        tail_low = tail - tail_high
        tails = jnp.concatenate(
            [tail_high, tail_low, tail_high, jnp.zeros((DEPTH - 3 * cells - 24, CHUNK), jnp.float32)], axis=0
        ).astype(jnp.bfloat16)
        return jnp.concatenate([high, low, high, tails], axis=0)

    time_step = COURANT / jnp.max(jnp.max(rates[...], axis=0, keepdims=True), axis=1, keepdims=True)
    scaled = source[...] * (1.0 / stretch)
    lead = message_one[12:16, :]
    row = lax.broadcasted_iota(jnp.int32, lead.shape, 0)
    lead = jnp.where(row == 1, offset[...], lead)
    tail = jnp.concatenate([lead, message_two[12:16, :]], axis=0)
    velocity_x = jnp.dot(drift[...], stacked(scaled, tail), preferred_element_type=jnp.float32)
    speed = velocity[...]
    for k in range(3):
        field = fields[k]
        tail = jnp.concatenate([message_one[4 * k : 4 * k + 4, :], message_two[4 * k : 4 * k + 4, :]], axis=0)
        weights = mixed if k < 2 else mixed_scalar
        both = jnp.dot(weights[...], stacked(field, tail), preferred_element_type=jnp.float32)
        tendency = both[cells:] - (speed * both[:cells] + field * velocity_x)
        updated = KEEP_FACTOR * register[k] + time_step * tendency
        new_register[k] = updated
        new_fields[k] = field + STEP_FACTOR * updated


def local(fields, register, source, metric, curvature):
    cells, lines = source.shape
    steps = lines // CHUNK
    count = lax.axis_size(("slab", "inner"))
    inner_count, slab_count = lax.axis_size("inner"), lax.axis_size("slab")
    devices = count * lax.axis_size("gz")
    inner, slab = lax.axis_index("inner"), lax.axis_index("slab")
    position = slab * inner_count + inner
    kind = jnp.where(position == 0, 0, jnp.where(position == count - 1, 3, 1 + position % 2))
    where = jnp.reshape(kind, (1,)).astype(jnp.int32)
    place = jnp.stack([inner, slab]).astype(jnp.int32)
    send_weights, solve_tables = tables(cells)
    metric_row, curvature_row = metric[None, :], curvature[None, :]

    by_field = pl.BlockSpec((3, cells, CHUNK), lambda i, s: (0, 0, i))
    by_line = pl.BlockSpec((cells, CHUNK), lambda i, s: (0, i))
    by_row = pl.BlockSpec((1, cells), lambda i, s: (0, 0))
    by_message = pl.BlockSpec((MESSAGE, CHUNK), lambda i, s: (0, i))
    by_total = pl.BlockSpec((inner_count, CHUNK // LANES, LANES), lambda i, s: (0, i, 0))
    by_slab = pl.BlockSpec((slab_count, CHUNK // LANES, LANES), lambda i, s: (0, i, 0))
    by_offset = pl.BlockSpec((1, CHUNK), lambda i, s: (0, i))

    def shape(*sizes):
        return jax.ShapeDtypeStruct(sizes, jnp.float32)

    totals, message_one, message_two = pl.pallas_call(
        send_kernel,
        grid_spec=pltpu.PrefetchScalarGridSpec(
            num_scalar_prefetch=1,
            grid=(steps,),
            in_specs=[by_field, by_line, by_row, pl.BlockSpec((1, cells, LANES), lambda i, s: (s[0], 0, 0))],
            out_specs=[by_total, by_message, by_message],
        ),
        out_shape=[shape(inner_count, lines // LANES, LANES), shape(MESSAGE, lines), shape(MESSAGE, lines)],
        name="send",
    )(where, fields, source, metric_row, jnp.asarray(send_weights))

    line = ("slab", "inner")
    even_pairs = [(i, i ^ 1) for i in range(count)]
    odd_pairs = [(i, i + 1 if i % 2 else i - 1) for i in range(1, count - 1)]
    got_one = lax.ppermute(message_one, line, even_pairs)
    got_two = lax.ppermute(message_two, line, odd_pairs)

    inner_totals = lax.all_to_all(totals, "inner", 0, 0)
    slab_total = jnp.sum(inner_totals, axis=0, keepdims=True)
    slab_totals = lax.all_to_all(jnp.broadcast_to(slab_total, (slab_count, *slab_total.shape[1:])), "slab", 0, 0)

    lower = np.tril(np.ones((cells, cells))) - 0.5 * np.eye(cells)
    lower = jnp.asarray(np.concatenate([lower] * 3, axis=1), jnp.bfloat16)
    velocity, offset, rate = pl.pallas_call(
        velocity_kernel,
        grid_spec=pltpu.PrefetchScalarGridSpec(
            num_scalar_prefetch=1,
            grid=(steps,),
            in_specs=[by_line, by_row, by_total, by_slab, pl.BlockSpec((cells, 3 * cells), lambda i, s: (0, 0))],
            out_specs=[by_line, by_offset, pl.BlockSpec((devices, LANES), lambda i, s: (0, 0))],
            scratch_shapes=[pltpu.VMEM((8, LANES), jnp.float32)],
        ),
        out_shape=[shape(cells, lines), shape(1, lines), shape(devices, LANES)],
        name="velocity",
    )(place, source, metric_row, inner_totals, slab_totals, lower)

    rates = lax.all_to_all(rate, ("slab", "inner", "gz"), 0, 0, tiled=True)

    new_fields, new_register = pl.pallas_call(
        update_kernel,
        grid_spec=pltpu.PrefetchScalarGridSpec(
            num_scalar_prefetch=1,
            grid=(steps,),
            in_specs=[
                by_field, by_field, by_line, by_line, by_offset, by_message, by_message, by_row, by_row,
                pl.BlockSpec((devices, LANES), lambda i, s: (0, 0)),
                pl.BlockSpec((1, 3, cells, DEPTH), lambda i, s: (s[0], 0, 0, 0)),
            ],
            out_specs=[by_field, by_field],
            scratch_shapes=[
                pltpu.VMEM((2 * cells, DEPTH), jnp.bfloat16),
                pltpu.VMEM((2 * cells, DEPTH), jnp.bfloat16),
                pltpu.VMEM((cells, DEPTH), jnp.bfloat16),
            ],
        ),
        out_shape=[shape(3, cells, lines), shape(3, cells, lines)],
        compiler_params=pltpu.CompilerParams(vmem_limit_bytes=32 * 1024 * 1024),
        name="update",
    )(
        where, fields, register, source, velocity, offset, got_one, got_two, metric_row, curvature_row, rates,
        jnp.asarray(solve_tables),
    )
    return (new_fields, new_register, velocity)


def solution(mesh):
    along, across = mesh.devices.shape
    inner = 1
    while inner * inner < along:
        inner *= 2
    split = Mesh(mesh.devices.reshape(along // inner, inner, across), ("slab", "inner", "gz"))
    line = ("slab", "inner")
    placed = (P(None, line, "gz"), P(None, line, "gz"), P(line, "gz"), P(line), P(line))
    return jax.shard_map(
        local,
        mesh=split,
        in_specs=placed,
        out_specs=(P(None, line, "gz"), P(None, line, "gz"), P(line, "gz")),
        check_vma=False,
    )
```

```python
import functools

import jax
import jax.numpy as jnp
import numpy as np
from jax import lax
from jax.experimental import pallas as pl
from jax.experimental.pallas import tpu as pltpu
from jax.sharding import Mesh
from jax.sharding import PartitionSpec as P

ALPHA_ONE = 1.0 / 3.0
COEF_ONE = 14.0 / 9.0
WIDE_ONE = 1.0 / 9.0
ALPHA_TWO = 2.0 / 11.0
COEF_TWO = 12.0 / 11.0
WIDE_TWO = 3.0 / 11.0
VISCOSITY = 0.25
DIFFUSIVITY = 0.2
COURANT = 1.2
KEEP_FACTOR = -5.0 / 9.0
STEP_FACTOR = 15.0 / 16.0

LANES = 128
CHUNK = 1024
GRANT = 24 * 1024 * 1024
MESSAGE = 16
DEPTH = 256


def inverse(alpha, length):
    matrix = np.eye(length) + alpha * (np.eye(length, k=1) + np.eye(length, k=-1))
    return np.linalg.inv(matrix)


@functools.cache
def operators(cells):
    length = 4 * cells
    near_up, near_down = np.eye(length, k=1), np.eye(length, k=-1)
    far_up, far_down = np.eye(length, k=2), np.eye(length, k=-2)
    first = COEF_ONE / 2.0 * (near_up - near_down) + WIDE_ONE / 4.0 * (far_up - far_down)
    second = COEF_TWO * (near_up - 2.0 * np.eye(length) + near_down) + WIDE_TWO / 4.0 * (
        far_up - 2.0 * np.eye(length) + far_down
    )
    slope = inverse(ALPHA_ONE, length) @ first
    bend = inverse(ALPHA_TWO, length) @ second
    integral = -(np.tril(np.ones((length, length))) - 0.5 * np.eye(length))
    constant = slope @ np.ones(length)
    return slope, bend, slope @ integral, constant


def from_left(matrix, block, cells):
    start = block * cells
    part = matrix[start : start + cells, start - cells : start]
    weights = part[1]
    factors = part[:, cells - 2] / part[1, cells - 2]
    corner = np.zeros(cells)
    corner[0] = part[0, cells - 1] - factors[0] * part[1, cells - 1]
    return factors, weights, corner


def from_right(matrix, block, cells):
    start = block * cells
    part = matrix[start : start + cells, start + cells : start + 2 * cells]
    weights = part[cells - 2]
    factors = part[:, 1] / part[cells - 2, 1]
    corner = np.zeros(cells)
    corner[cells - 1] = part[cells - 1, 0] - factors[cells - 1] * part[cells - 2, 0]
    return factors, weights, corner


@functools.cache
def tables(cells):
    slope, bend, drift, constant = operators(cells)
    kinds = (0, 2, 1, 3)
    send = np.zeros((4, cells, LANES))
    solve = np.zeros((4, 3, cells, DEPTH))
    for kind, block in enumerate(kinds):
        odd = kind >= 2
        start = block * cells
        own = slice(start, start + cells)
        rest = np.zeros(4 * cells)
        if block == 3:
            rest[own] = constant[own]
        local = drift + rest[:, None] * (np.arange(4 * cells) < start)[None, :]
        for which, matrix in enumerate((slope, bend, local)):
            base = np.zeros((cells, cells + 8))
            base[:, :cells] = matrix[own, own]
            left, right = (0, 4) if odd else (4, 0)
            slot = 1 if which == 1 else 0
            if block > 0:
                factors, _, corner = from_left(matrix, block, cells)
                base[:, cells + left + slot] = factors
                base[:, cells + left + 2] = corner
            if block < 3:
                factors, _, corner = from_right(matrix, block, cells)
                base[:, cells + right + slot] = factors
                base[:, cells + right + 2] = corner
            if which == 2:
                base[:, cells + 1] = -rest[own]
            for copy in range(3):
                solve[kind, which, :, copy * cells : (copy + 1) * cells] = base[:, :cells]
                solve[kind, which, :, 3 * cells + 8 * copy : 3 * cells + 8 * copy + 8] = base[:, cells:]
            to_right = to_left = np.zeros(cells)
            sent = (slope, bend, drift)[which]
            if block < 2:
                to_right = from_left(sent, block + 1, cells)[1]
            elif block == 2:
                to_right = from_left(sent, 2, cells)[1]
            if block > 0:
                to_left = from_right(sent, block - 1, cells)[1]
            pair = (to_left, to_right) if odd else (to_right, to_left)
            send[kind, :, which] = pair[0]
            send[kind, :, 3 + which] = pair[1]
    return send.astype(np.float32), solve.astype(np.float32)


def column(row):
    size = row.shape[1]
    rows = lax.broadcasted_iota(jnp.int32, (size, size), 0)
    columns = lax.broadcasted_iota(jnp.int32, (size, size), 1)
    spread = jnp.broadcast_to(row, (size, size))
    return jnp.sum(jnp.where(rows == columns, spread, 0.0), axis=1, keepdims=True)


def halves(value):
    high = value.astype(jnp.bfloat16)
    low = (value - high.astype(jnp.float32)).astype(jnp.bfloat16)
    return high, low


def pieces_of(lines):
    return [slice(start, start + CHUNK) for start in range(0, lines, CHUNK)]


def totals_kernel(source, metric, totals, held, held_metric, sems):
    pieces = pieces_of(source.shape[1])
    metric_copy = pltpu.make_async_copy(metric, held_metric, sems.at[len(pieces)])
    metric_copy.start()
    copies = [pltpu.make_async_copy(source.at[:, p], held.at[:, p], sems.at[i]) for i, p in enumerate(pieces)]
    for copy in copies:
        copy.start()
    metric_copy.wait()
    scale = 1.0 / column(held_metric[...])
    for i, p in enumerate(pieces):
        copies[i].wait()
        total = jnp.sum(held[:, p] * scale, axis=0, keepdims=True)
        for peer in range(totals.shape[0]):
            for k in range(CHUNK // LANES):
                row = i * (CHUNK // LANES) + k
                totals[peer, row : row + 1, :] = total[:, k * LANES : (k + 1) * LANES]


def send_kernel(
    kind, fields, source, metric, weights, message_one, message_two, held, held_source, held_metric, held_weights, sems
):
    cells, lines = source.shape
    pieces = pieces_of(lines)
    metric_copy = pltpu.make_async_copy(metric, held_metric, sems.at[2, 0])
    metric_copy.start()
    weights_copy = pltpu.make_async_copy(weights.at[kind[0]], held_weights, sems.at[2, 1])
    weights_copy.start()
    copies = []
    for i, p in enumerate(pieces):
        pair = (
            pltpu.make_async_copy(fields.at[:, :, p], held.at[:, :, p], sems.at[0, i]),
            pltpu.make_async_copy(source.at[:, p], held_source.at[:, p], sems.at[1, i]),
        )
        for copy in pair:
            copy.start()
        copies.append(pair)
    odd = kind[0] >= 2
    metric_copy.wait()
    weights_copy.wait()
    chosen = held_weights[...]
    scale = 1.0 / column(held_metric[...])
    blank = jnp.zeros((1, CHUNK), jnp.float32)
    for i, p in enumerate(pieces):
        for copy in copies[i]:
            copy.wait()
        for k in range(4):
            value = held[k, :, p] if k < 3 else held_source[:, p] * scale
            first, last = value[:1], value[cells - 1 :]
            for message, begin in ((message_one, 0), (message_two, 3)):
                row = 4 * k
                if k < 3:
                    for which in range(2):
                        weight = chosen[:, begin + which : begin + which + 1]
                        message[row + which : row + which + 1, p] = jnp.sum(value * weight, axis=0, keepdims=True)
                else:
                    weight = chosen[:, begin + 2 : begin + 3]
                    message[row : row + 1, p] = jnp.sum(value * weight, axis=0, keepdims=True)
                    message[row + 1 : row + 2, p] = blank
                edge = jnp.where(odd, first, last) if begin == 0 else jnp.where(odd, last, first)
                message[row + 2 : row + 3, p] = edge
                message[row + 3 : row + 4, p] = blank


def slab_kernel(inner, after_one, after_two, sums):
    del after_one, after_two
    total = inner[0]
    for peer in range(1, inner.shape[0]):
        total += inner[peer]
    for peer in range(sums.shape[0]):
        sums[peer] = total


def running_kernel(after, source, metric, lower, running, spread, held, held_metric, sems):
    del after
    pieces = pieces_of(source.shape[1])
    metric_copy = pltpu.make_async_copy(metric, held_metric, sems.at[len(pieces)])
    metric_copy.start()
    copies = [pltpu.make_async_copy(source.at[:, p], held.at[:, p], sems.at[i]) for i, p in enumerate(pieces)]
    for copy in copies:
        copy.start()
    metric_copy.wait()
    stretch = column(held_metric[...])
    spread[...] = jnp.broadcast_to(stretch, spread.shape)
    scale = 1.0 / stretch
    for i, p in enumerate(pieces):
        copies[i].wait()
        scaled = held[:, p] * scale
        high = scaled.astype(jnp.bfloat16)
        rest = scaled - high.astype(jnp.float32)
        middle = rest.astype(jnp.bfloat16)
        low = (rest - middle.astype(jnp.float32)).astype(jnp.bfloat16)
        stacked = jnp.concatenate([high, middle, low], axis=0)
        running[:, p] = jnp.dot(lower[...], stacked, preferred_element_type=jnp.float32)


def velocity_kernel(place, slab, running, spread, inner, outer, velocity, offset, rate):
    stretch = spread[...]
    squared = 4.0 * VISCOSITY * stretch * stretch
    before = jnp.zeros(inner.shape[1:], jnp.float32)
    for peer in range(inner.shape[0]):
        before += jnp.where(peer < place[0], inner[peer], 0.0)
    for peer in range(outer.shape[0]):
        before += jnp.where(peer < slab[0], outer[peer], 0.0)
    top = jnp.zeros((1, LANES), jnp.float32)
    for k in range(before.shape[0]):
        here = slice(k * LANES, (k + 1) * LANES)
        shift = before[k : k + 1, :]
        offset[:, here] = shift
        value = -(running[:, here] + shift)
        velocity[:, here] = value
        top = jnp.maximum(top, jnp.max(jnp.abs(value) * stretch + squared, axis=0, keepdims=True))
    peak = jnp.max(top, axis=1, keepdims=True)
    rate[...] = jnp.broadcast_to(peak, rate.shape)


def tendency_kernel(
    kind, fields, source, velocity, offset, spread, message_one, message_two, curvature, table,
    tendency, velocity_out,
    held_fields, held_source, held_table, held_curvature, mixed, mixed_scalar, drift, sems,
):
    cells, lines = source.shape
    pieces = pieces_of(lines)
    table_copy = pltpu.make_async_copy(table.at[kind[0]], held_table, sems.at[2, 0])
    table_copy.start()
    curvature_copy = pltpu.make_async_copy(curvature, held_curvature, sems.at[2, 1])
    curvature_copy.start()
    copies = []
    for i, p in enumerate(pieces):
        group = (
            pltpu.make_async_copy(source.at[:, p], held_source.at[:, p], sems.at[0, i]),
            pltpu.make_async_copy(fields.at[:, :, p], held_fields.at[:, :, p], sems.at[1, i]),
        )
        for copy in group:
            copy.start()
        copies.append(group)
    out_copy = pltpu.make_async_copy(velocity, velocity_out, sems.at[2, 2])
    out_copy.start()

    stretch = spread[:, :1]
    table_copy.wait()
    curvature_copy.wait()
    curving = column(held_curvature[...])
    slope, bend = held_table[0], held_table[1]
    lane = lax.broadcasted_iota(jnp.int32, (cells, DEPTH), 1)
    is_low = ((lane >= 2 * cells) & (lane < 3 * cells)) | (lane >= 3 * cells + 16)

    def split(value):
        high, low = halves(value)
        return jnp.where(is_low, low.astype(jnp.float32), high.astype(jnp.float32)).astype(jnp.bfloat16)

    field_x = stretch * slope
    field_xx = stretch * stretch * bend + curving * slope
    mixed[:cells, :] = split(field_x)
    mixed[cells:, :] = split(VISCOSITY * field_xx)
    mixed_scalar[:cells, :] = mixed[:cells, :]
    mixed_scalar[cells:, :] = split(DIFFUSIVITY * field_xx)
    drift[...] = split(stretch * held_table[2])

    def stacked(value, tail):
        high, low = halves(value)
        tail_high = tail.astype(jnp.bfloat16).astype(jnp.float32)
        tail_low = tail - tail_high
        tails = jnp.concatenate(
            [tail_high, tail_low, tail_high, jnp.zeros((DEPTH - 3 * cells - 24, CHUNK), jnp.float32)], axis=0
        ).astype(jnp.bfloat16)
        return jnp.concatenate([high, low, high, tails], axis=0)

    for i, p in enumerate(pieces):
        copies[i][0].wait()
        scaled = held_source[:, p] * (1.0 / stretch)
        lead = message_one[12:16, p]
        row = lax.broadcasted_iota(jnp.int32, lead.shape, 0)
        lead = jnp.where(row == 1, offset[:, p], lead)
        tail = jnp.concatenate([lead, message_two[12:16, p]], axis=0)
        velocity_x = jnp.dot(drift[...], stacked(scaled, tail), preferred_element_type=jnp.float32)
        speed = velocity[:, p]
        copies[i][1].wait()
        for k in range(3):
            field = held_fields[k, :, p]
            tail = jnp.concatenate([message_one[4 * k : 4 * k + 4, p], message_two[4 * k : 4 * k + 4, p]], axis=0)
            weights = mixed if k < 2 else mixed_scalar
            both = jnp.dot(weights[...], stacked(field, tail), preferred_element_type=jnp.float32)
            tendency[k, :, p] = both[cells:] - (speed * both[:cells] + field * velocity_x)
    out_copy.wait()


def update_kernel(fields, register, tendency, rates, new_fields, new_register, held_fields, held_register, sems):
    pieces = [(k, p) for k in range(3) for p in pieces_of(tendency.shape[2])]
    arrivals = []
    for i, (k, p) in enumerate(pieces):
        pair = (
            pltpu.make_async_copy(register.at[k, :, p], held_register.at[k, :, p], sems.at[0, i]),
            pltpu.make_async_copy(fields.at[k, :, p], held_fields.at[k, :, p], sems.at[1, i]),
        )
        for copy in pair:
            copy.start()
        arrivals.append(pair)
    time_step = COURANT / jnp.max(jnp.max(rates[...], axis=0, keepdims=True), axis=1, keepdims=True)
    departures = []
    for i, (k, p) in enumerate(pieces):
        arrivals[i][0].wait()
        updated = KEEP_FACTOR * held_register[k, :, p] + time_step * tendency[k, :, p]
        held_register[k, :, p] = updated
        departures.append(pltpu.make_async_copy(held_register.at[k, :, p], new_register.at[k, :, p], sems.at[2, i]))
        departures[-1].start()
        arrivals[i][1].wait()
        held_fields[k, :, p] = held_fields[k, :, p] + STEP_FACTOR * updated
        departures.append(pltpu.make_async_copy(held_fields.at[k, :, p], new_fields.at[k, :, p], sems.at[3, i]))
        departures[-1].start()
    for copy in departures:
        copy.wait()


def local(fields, register, source, metric, curvature):
    cells, lines = source.shape
    steps = lines // CHUNK
    groups = lines // LANES
    inner_count, slab_count = lax.axis_size("inner"), lax.axis_size("slab")
    count = inner_count * slab_count
    devices = count * lax.axis_size("gz")
    inner, slab = lax.axis_index("inner"), lax.axis_index("slab")
    position = slab * inner_count + inner
    kind = jnp.where(position == 0, 0, jnp.where(position == count - 1, 3, 1 + position % 2))
    kind, inner, slab = (jnp.reshape(value, (1,)).astype(jnp.int32) for value in (kind, inner, slab))
    send_weights, solve_tables = tables(cells)
    metric_row, curvature_row = metric[None, :], curvature[None, :]

    smem = pl.BlockSpec(memory_space=pltpu.SMEM)
    vmem = pl.BlockSpec(memory_space=pltpu.VMEM)
    hbm = pl.BlockSpec(memory_space=pl.ANY)

    def shape(*sizes):
        return jax.ShapeDtypeStruct(sizes, jnp.float32)

    def fast(*sizes):
        return pltpu.VMEM(sizes, jnp.float32)

    def keep(value):
        return pltpu.with_memory_space_constraint(value, pltpu.VMEM)

    def far(value):
        return pltpu.with_memory_space_constraint(value, pltpu.HBM)

    def cost(bytes_accessed, flops=0):
        return pl.CostEstimate(flops=flops, bytes_accessed=bytes_accessed, transcendentals=0)

    params = pltpu.CompilerParams(vmem_limit_bytes=GRANT)
    line_bytes = 4 * cells * lines
    source, fields, register = far(source), far(fields), far(register)
    metric_row, curvature_row = far(metric_row), far(curvature_row)
    semaphores = pltpu.SemaphoreType.DMA
    one_row = fast(1, cells)

    totals = pl.pallas_call(
        totals_kernel,
        in_specs=[hbm, hbm],
        out_specs=vmem,
        out_shape=fast(inner_count, groups, LANES),
        scratch_shapes=[fast(cells, lines), one_row, semaphores((steps + 1,))],
        compiler_params=params,
        cost_estimate=cost(line_bytes),
        name="totals",
    )(source, metric_row)
    inner_totals = lax.all_to_all(totals, "inner", 0, 0)

    message_one, message_two = pl.pallas_call(
        send_kernel,
        in_specs=[smem, hbm, hbm, hbm, hbm],
        out_specs=[vmem, vmem],
        out_shape=[fast(MESSAGE, lines), fast(MESSAGE, lines)],
        scratch_shapes=[fast(3, cells, lines), fast(cells, lines), one_row, fast(cells, LANES), semaphores((3, max(steps, 2)))],
        compiler_params=params,
        cost_estimate=cost(4 * line_bytes),
        name="send",
    )(kind, fields, source, metric_row, far(jnp.asarray(send_weights)))

    slab_sums = pl.pallas_call(
        slab_kernel,
        in_specs=[vmem, hbm, hbm],
        out_specs=vmem,
        out_shape=fast(slab_count, groups, LANES),
        compiler_params=params,
        name="slab",
    )(keep(inner_totals), message_one, message_two)
    slab_totals = lax.all_to_all(slab_sums, "slab", 0, 0)

    line = ("slab", "inner")
    even_pairs = [(i, i ^ 1) for i in range(count)]
    odd_pairs = [(i, i + 1 if i % 2 else i - 1) for i in range(1, count - 1)]
    got_one = lax.ppermute(message_one, line, even_pairs)
    got_two = lax.ppermute(message_two, line, odd_pairs)

    lower = np.tril(np.ones((cells, cells))) - 0.5 * np.eye(cells)
    lower = jnp.asarray(np.concatenate([lower] * 3, axis=1), jnp.bfloat16)
    running, spread = pl.pallas_call(
        running_kernel,
        in_specs=[hbm, hbm, hbm, vmem],
        out_specs=[vmem, vmem],
        out_shape=[fast(cells, lines), fast(cells, LANES)],
        scratch_shapes=[fast(cells, lines), one_row, semaphores((steps + 1,))],
        compiler_params=params,
        cost_estimate=cost(2 * line_bytes),
        name="running",
    )(slab_sums, source, metric_row, lower)

    velocity, offset, rate = pl.pallas_call(
        velocity_kernel,
        in_specs=[smem, smem, vmem, vmem, vmem, vmem],
        out_specs=[vmem, vmem, vmem],
        out_shape=[fast(cells, lines), fast(1, lines), fast(devices, LANES)],
        compiler_params=params,
        cost_estimate=cost(2 * line_bytes),
        name="velocity",
    )(inner, slab, keep(running), keep(spread), keep(inner_totals), keep(slab_totals))

    rates = lax.all_to_all(rate, ("slab", "inner", "gz"), 0, 0, tiled=True)

    tendency, velocity_out = pl.pallas_call(
        tendency_kernel,
        in_specs=[smem, hbm, hbm, vmem, vmem, vmem, vmem, vmem, hbm, hbm],
        out_specs=[vmem, hbm],
        out_shape=[fast(3, cells, lines), pltpu.HBM((cells, lines), jnp.float32)],
        scratch_shapes=[
            fast(3, cells, lines),
            fast(cells, lines),
            fast(3, cells, DEPTH),
            one_row,
            pltpu.VMEM((2 * cells, DEPTH), jnp.bfloat16),
            pltpu.VMEM((2 * cells, DEPTH), jnp.bfloat16),
            pltpu.VMEM((cells, DEPTH), jnp.bfloat16),
            semaphores((3, max(steps, 3))),
        ],
        compiler_params=params,
        cost_estimate=cost(12 * line_bytes),
        name="tendency",
    )(
        kind, fields, source, keep(velocity), keep(offset), keep(spread), got_one, got_two, curvature_row,
        far(jnp.asarray(solve_tables)),
    )

    new_fields, new_register = pl.pallas_call(
        update_kernel,
        in_specs=[hbm, hbm, vmem, vmem],
        out_specs=[hbm, hbm],
        out_shape=[pltpu.HBM((3, cells, lines), jnp.float32)] * 2,
        scratch_shapes=[fast(3, cells, lines), fast(3, cells, lines), semaphores((4, 3 * steps))],
        compiler_params=params,
        cost_estimate=cost(12 * line_bytes),
        name="update",
    )(fields, register, keep(tendency), rates)
    return (new_fields, new_register, velocity_out)


def solution(mesh):
    along, across = mesh.devices.shape
    inner = 1
    while inner * inner < along:
        inner *= 2
    split = Mesh(mesh.devices.reshape(along // inner, inner, across), ("slab", "inner", "gz"))
    line = ("slab", "inner")
    placed = (P(None, line, "gz"), P(None, line, "gz"), P(line, "gz"), P(line), P(line))
    return jax.shard_map(
        local,
        mesh=split,
        in_specs=placed,
        out_specs=(P(None, line, "gz"), P(None, line, "gz"), P(line, "gz")),
        check_vma=False,
    )
```

```python
import functools

import jax
import jax.numpy as jnp
import numpy as np
from jax import lax
from jax.experimental import pallas as pl
from jax.experimental.pallas import tpu as pltpu
from jax.sharding import Mesh
from jax.sharding import PartitionSpec as P

ALPHA_ONE = 1.0 / 3.0
COEF_ONE = 14.0 / 9.0
WIDE_ONE = 1.0 / 9.0
ALPHA_TWO = 2.0 / 11.0
COEF_TWO = 12.0 / 11.0
WIDE_TWO = 3.0 / 11.0
VISCOSITY = 0.25
DIFFUSIVITY = 0.2
COURANT = 1.2
KEEP_FACTOR = -5.0 / 9.0
STEP_FACTOR = 15.0 / 16.0

LANES = 128
STEPS = 4
GRANT = 24 * 1024 * 1024
MESSAGE = 11
DEPTH = 256


def inverse(alpha, length):
    matrix = np.eye(length) + alpha * (np.eye(length, k=1) + np.eye(length, k=-1))
    return np.linalg.inv(matrix)


@functools.cache
def operators(cells):
    length = 4 * cells
    near_up, near_down = np.eye(length, k=1), np.eye(length, k=-1)
    far_up, far_down = np.eye(length, k=2), np.eye(length, k=-2)
    first = COEF_ONE / 2.0 * (near_up - near_down) + WIDE_ONE / 4.0 * (far_up - far_down)
    second = COEF_TWO * (near_up - 2.0 * np.eye(length) + near_down) + WIDE_TWO / 4.0 * (
        far_up - 2.0 * np.eye(length) + far_down
    )
    slope = inverse(ALPHA_ONE, length) @ first
    bend = inverse(ALPHA_TWO, length) @ second
    integral = -(np.tril(np.ones((length, length))) - 0.5 * np.eye(length))
    constant = slope @ np.ones(length)
    return slope, bend, slope @ integral, constant


def from_left(matrix, block, cells):
    start = block * cells
    part = matrix[start : start + cells, start - cells : start]
    weights = part[1]
    factors = part[:, cells - 2] / part[1, cells - 2]
    corner = np.zeros(cells)
    corner[0] = part[0, cells - 1] - factors[0] * part[1, cells - 1]
    return factors, weights, corner


def from_right(matrix, block, cells):
    start = block * cells
    part = matrix[start : start + cells, start + cells : start + 2 * cells]
    weights = part[cells - 2]
    factors = part[:, 1] / part[cells - 2, 1]
    corner = np.zeros(cells)
    corner[cells - 1] = part[cells - 1, 0] - factors[cells - 1] * part[cells - 2, 0]
    return factors, weights, corner


@functools.cache
def tables(cells):
    slope, bend, drift, constant = operators(cells)
    kinds = (0, 2, 1, 3)
    send = np.zeros((4, cells, LANES))
    solve = np.zeros((4, 3, cells, DEPTH))
    for kind, block in enumerate(kinds):
        odd = kind >= 2
        start = block * cells
        own = slice(start, start + cells)
        rest = np.zeros(4 * cells)
        if block == 3:
            rest[own] = constant[own]
        local = drift + rest[:, None] * (np.arange(4 * cells) < start)[None, :]
        for which, matrix in enumerate((slope, bend, local)):
            base = np.zeros((cells, cells + 8))
            base[:, :cells] = matrix[own, own]
            left, right = (0, 4) if odd else (4, 0)
            slot = 1 if which == 1 else 0
            if block > 0:
                factors, _, corner = from_left(matrix, block, cells)
                base[:, cells + left + slot] = factors
                base[:, cells + left + 2] = corner
            if block < 3:
                factors, _, corner = from_right(matrix, block, cells)
                base[:, cells + right + slot] = factors
                base[:, cells + right + 2] = corner
            if which == 2:
                base[:, cells + 1] = -rest[own]
            for copy in range(3):
                solve[kind, which, :, copy * cells : (copy + 1) * cells] = base[:, :cells]
                solve[kind, which, :, 3 * cells + 8 * copy : 3 * cells + 8 * copy + 8] = base[:, cells:]
            to_right = to_left = np.zeros(cells)
            sent = (slope, bend, drift)[which]
            if block < 2:
                to_right = from_left(sent, block + 1, cells)[1]
            elif block == 2:
                to_right = from_left(sent, 2, cells)[1]
            if block > 0:
                to_left = from_right(sent, block - 1, cells)[1]
            pair = (to_left, to_right) if odd else (to_right, to_left)
            send[kind, :, which] = pair[0]
            send[kind, :, 3 + which] = pair[1]
    return send.astype(np.float32), solve.astype(np.float32)


def column(row):
    size = row.shape[1]
    rows = lax.broadcasted_iota(jnp.int32, (size, size), 0)
    columns = lax.broadcasted_iota(jnp.int32, (size, size), 1)
    spread = jnp.broadcast_to(row, (size, size))
    return jnp.sum(jnp.where(rows == columns, spread, 0.0), axis=1, keepdims=True)


def halves(value):
    high = value.astype(jnp.bfloat16)
    low = (value - high.astype(jnp.float32)).astype(jnp.bfloat16)
    return high, low


def pieces_of(lines, count=STEPS):
    width = lines // count
    return [slice(start, start + width) for start in range(0, lines, width)]


def message_shape(lines):
    return 8, lines + (MESSAGE - 8) * (lines // 8)


def put(message, row, part, value):
    width = value.shape[1]
    fold = width // 2
    if row < 8:
        message[row : row + 1, part * width : (part + 1) * width] = value
        return
    start = STEPS * width + (row - 8) * fold
    for half in range(2):
        line = 2 * part + half
        message[line : line + 1, start : start + fold] = value[:, half * fold : (half + 1) * fold]


def take(message, row, part, width):
    fold = width // 2
    if row < 8:
        return message[row : row + 1, part * width : (part + 1) * width]
    start = STEPS * width + (row - 8) * fold
    return jnp.concatenate(
        [message[2 * part + half : 2 * part + half + 1, start : start + fold] for half in range(2)], axis=1
    )


def totals_kernel(source, metric, totals, held, held_metric, sems):
    cells, lines = source.shape
    metric_copy = pltpu.make_async_copy(metric, held_metric, sems.at[2])
    metric_copy.start()
    rows = [slice(0, cells // 2), slice(cells // 2, cells)]
    copies = [pltpu.make_async_copy(source.at[r, :], held.at[r, :], sems.at[i]) for i, r in enumerate(rows)]
    for copy in copies:
        copy.start()
    metric_copy.wait()
    scale = 1.0 / column(held_metric[...])
    total = jnp.zeros((1, lines), jnp.float32)
    for copy, r in zip(copies, rows):
        copy.wait()
        total += jnp.sum(held[r, :] * scale[r], axis=0, keepdims=True)
    for peer in range(totals.shape[0]):
        for k in range(lines // LANES):
            totals[peer, k : k + 1, :] = total[:, k * LANES : (k + 1) * LANES]


def send_kernel(
    kind, fields, source, metric, weights, lower, message_one, message_two, running, spread,
    held, held_source, held_metric, held_weights, held_lower, sems,
):
    cells, lines = source.shape
    pieces = pieces_of(lines, STEPS // 2)
    metric_copy = pltpu.make_async_copy(metric, held_metric, sems.at[2, 0])
    metric_copy.start()
    weights_copy = pltpu.make_async_copy(weights.at[kind[0]], held_weights, sems.at[2, 1])
    weights_copy.start()
    lower_copy = pltpu.make_async_copy(lower, held_lower, sems.at[2, 2])
    lower_copy.start()
    copies = []
    for i, p in enumerate(pieces):
        pair = (
            pltpu.make_async_copy(source.at[:, p], held_source.at[:, p], sems.at[1, i]),
            pltpu.make_async_copy(fields.at[:, :, p], held.at[:, :, p], sems.at[0, i]),
        )
        for copy in pair:
            copy.start()
        copies.append(pair)
    odd = kind[0] >= 2
    metric_copy.wait()
    weights_copy.wait()
    lower_copy.wait()
    chosen = held_weights[...]
    stretch = column(held_metric[...])
    spread[...] = jnp.broadcast_to(stretch, spread.shape)
    scale = 1.0 / stretch
    for i, p in enumerate(pieces_of(lines)):
        if i % 2 == 0:
            for copy in copies[i // 2]:
                copy.wait()
        scaled = held_source[:, p] * scale
        high = scaled.astype(jnp.bfloat16)
        rest = scaled - high.astype(jnp.float32)
        middle = rest.astype(jnp.bfloat16)
        low = (rest - middle.astype(jnp.float32)).astype(jnp.bfloat16)
        running[:, p] = jnp.dot(
            held_lower[...], jnp.concatenate([high, middle, low], axis=0), preferred_element_type=jnp.float32
        )
        for k in range(4):
            value = held[k, :, p] if k < 3 else scaled
            first, last = value[:1], value[cells - 1 :]
            for message, begin in ((message_one, 0), (message_two, 3)):
                row = 3 * k
                for which in range(2) if k < 3 else (2,):
                    weight = chosen[:, begin + which : begin + which + 1]
                    put(message, row, i, jnp.sum(value * weight, axis=0, keepdims=True))
                    row += 1
                put(message, row, i, jnp.where(odd, first, last) if begin == 0 else jnp.where(odd, last, first))


def slab_kernel(inner, after_one, after_two, sums):
    del after_one, after_two
    total = inner[0]
    for peer in range(1, inner.shape[0]):
        total += inner[peer]
    for peer in range(sums.shape[0]):
        sums[peer] = total


def velocity_kernel(place, slab, running, spread, inner, outer, velocity, offset, rate):
    stretch = spread[...]
    squared = 4.0 * VISCOSITY * stretch * stretch
    before = jnp.zeros(inner.shape[1:], jnp.float32)
    for peer in range(inner.shape[0]):
        before += jnp.where(peer < place[0], inner[peer], 0.0)
    for peer in range(outer.shape[0]):
        before += jnp.where(peer < slab[0], outer[peer], 0.0)
    top = jnp.zeros((1, LANES), jnp.float32)
    for k in range(before.shape[0]):
        here = slice(k * LANES, (k + 1) * LANES)
        shift = before[k : k + 1, :]
        offset[:, here] = shift
        value = -(running[:, here] + shift)
        velocity[:, here] = value
        top = jnp.maximum(top, jnp.max(jnp.abs(value) * stretch + squared, axis=0, keepdims=True))
    peak = jnp.max(top, axis=1, keepdims=True)
    rate[...] = jnp.broadcast_to(peak, rate.shape)


def inner_kernel(
    kind, fields, source, velocity, spread, curvature, table,
    partial, held_fields, edge_mixed, edge_scalar, edge_drift, velocity_out,
    held_source, held_table, held_curvature, mixed, mixed_scalar, drift, sems,
):
    cells, lines = source.shape
    table_copy = pltpu.make_async_copy(table.at[kind[0]], held_table, sems.at[2, 0])
    table_copy.start()
    curvature_copy = pltpu.make_async_copy(curvature, held_curvature, sems.at[2, 1])
    curvature_copy.start()
    copies = []
    for i, p in enumerate(pieces_of(lines, STEPS // 2)):
        group = (
            pltpu.make_async_copy(source.at[:, p], held_source.at[:, p], sems.at[0, i]),
            pltpu.make_async_copy(fields.at[:, :, p], held_fields.at[:, :, p], sems.at[1, i]),
        )
        for copy in group:
            copy.start()
        copies.append(group)
    out_copy = pltpu.make_async_copy(velocity, velocity_out, sems.at[2, 2])
    out_copy.start()

    stretch = spread[:, :1]
    table_copy.wait()
    curvature_copy.wait()
    curving = column(held_curvature[...])
    slope, bend = held_table[0], held_table[1]
    lane = lax.broadcasted_iota(jnp.int32, (cells, DEPTH), 1)
    is_low = ((lane >= 2 * cells) & (lane < 3 * cells)) | (lane >= 3 * cells + 16)

    def split(value):
        high, low = halves(value)
        return jnp.where(is_low, low.astype(jnp.float32), high.astype(jnp.float32))

    field_x = split(stretch * slope)
    field_xx = stretch * stretch * bend + curving * slope
    tables_of = (
        (mixed, edge_mixed, (field_x, split(VISCOSITY * field_xx))),
        (mixed_scalar, edge_scalar, (field_x, split(DIFFUSIVITY * field_xx))),
        (drift, edge_drift, (split(stretch * held_table[2]),)),
    )
    for whole, edge, values in tables_of:
        for n, value in enumerate(values):
            whole[n * cells : (n + 1) * cells, :] = value.astype(jnp.bfloat16)
            edge[n * cells : (n + 1) * cells, :] = value[:, 3 * cells :].astype(jnp.bfloat16)

    def stacked(value):
        high, low = halves(value)
        return jnp.concatenate([high, low, high], axis=0)

    depth = 3 * cells
    for i, p in enumerate(pieces_of(lines)):
        if i % 2 == 0:
            copies[i // 2][0].wait()
        scaled = held_source[:, p] * (1.0 / stretch)
        velocity_x = jnp.dot(drift[:, :depth], stacked(scaled), preferred_element_type=jnp.float32)
        speed = velocity[:, p]
        if i % 2 == 0:
            copies[i // 2][1].wait()
        for k in range(3):
            field = held_fields[k, :, p]
            weights = mixed if k < 2 else mixed_scalar
            both = jnp.dot(weights[:, :depth], stacked(field), preferred_element_type=jnp.float32)
            partial[k, :, p] = both[cells:] - (speed * both[:cells] + field * velocity_x)
    out_copy.wait()


def tendency_kernel(
    partial, fields, velocity, offset, edge_mixed, edge_scalar, edge_drift, message_one, message_two, tendency
):
    cells, lines = velocity.shape
    width = lines // STEPS
    blank = jnp.zeros((1, width), jnp.float32)
    zeros = jnp.zeros((edge_mixed.shape[1] - 24, width), jnp.float32)

    def tails(rows, part, second):
        found = [[blank if row is None else take(message, row, part, width) for row in rows] for message in (message_one, message_two)]
        tail = jnp.concatenate([found[0][0], found[0][1] if second is None else second, *found[0][2:], *found[1]], axis=0)
        high = tail.astype(jnp.bfloat16).astype(jnp.float32)
        return jnp.concatenate([high, tail - high, high, zeros], axis=0).astype(jnp.bfloat16)

    for i, p in enumerate(pieces_of(lines)):
        tail = tails((9, None, 10, None), i, offset[:, p])
        velocity_x = jnp.dot(edge_drift[...], tail, preferred_element_type=jnp.float32)
        speed = velocity[:, p]
        for k in range(3):
            tail = tails((3 * k, 3 * k + 1, 3 * k + 2, None), i, None)
            weights = edge_mixed if k < 2 else edge_scalar
            both = jnp.dot(weights[...], tail, preferred_element_type=jnp.float32)
            tendency[k, :, p] = partial[k, :, p] + (both[cells:] - (speed * both[:cells] + fields[k, :, p] * velocity_x))


def update_kernel(fields, register, tendency, rates, new_fields, new_register, held_fields, held_register, sems):
    cells = tendency.shape[1]
    edges = [0, 3 * cells // 8, 3 * cells // 4, cells]
    pieces = [(slice(None), slice(low, high)) for low, high in zip(edges[:-1], edges[1:])]
    arrivals = []
    for i, p in enumerate(pieces):
        pair = (
            pltpu.make_async_copy(register.at[p], held_register.at[p], sems.at[0, i]),
            pltpu.make_async_copy(fields.at[p], held_fields.at[p], sems.at[1, i]),
        )
        for copy in pair:
            copy.start()
        arrivals.append(pair)
    time_step = COURANT / jnp.max(jnp.max(rates[...], axis=0, keepdims=True), axis=1, keepdims=True)
    departures = []
    for i, p in enumerate(pieces):
        arrivals[i][0].wait()
        updated = KEEP_FACTOR * held_register[p] + time_step * tendency[p]
        held_register[p] = updated
        departures.append(pltpu.make_async_copy(held_register.at[p], new_register.at[p], sems.at[2, i]))
        departures[-1].start()
        arrivals[i][1].wait()
        held_fields[p] = held_fields[p] + STEP_FACTOR * updated
        departures.append(pltpu.make_async_copy(held_fields.at[p], new_fields.at[p], sems.at[3, i]))
        departures[-1].start()
    for copy in departures:
        copy.wait()


def local(fields, register, source, metric, curvature):
    cells, lines = source.shape
    groups = lines // LANES
    inner_count, slab_count = lax.axis_size("inner"), lax.axis_size("slab")
    count = inner_count * slab_count
    devices = count * lax.axis_size("gz")
    inner, slab = lax.axis_index("inner"), lax.axis_index("slab")
    position = slab * inner_count + inner
    kind = jnp.where(position == 0, 0, jnp.where(position == count - 1, 3, 1 + position % 2))
    kind, inner, slab = (jnp.reshape(value, (1,)).astype(jnp.int32) for value in (kind, inner, slab))
    send_weights, solve_tables = tables(cells)
    metric_row, curvature_row = metric[None, :], curvature[None, :]

    smem = pl.BlockSpec(memory_space=pltpu.SMEM)
    vmem = pl.BlockSpec(memory_space=pltpu.VMEM)
    hbm = pl.BlockSpec(memory_space=pl.ANY)

    def shape(*sizes):
        return jax.ShapeDtypeStruct(sizes, jnp.float32)

    def fast(*sizes):
        return pltpu.VMEM(sizes, jnp.float32)

    def keep(value):
        return pltpu.with_memory_space_constraint(value, pltpu.VMEM)

    def far(value):
        return pltpu.with_memory_space_constraint(value, pltpu.HBM)

    def cost(bytes_accessed, flops=0):
        return pl.CostEstimate(flops=flops, bytes_accessed=bytes_accessed, transcendentals=0)

    params = pltpu.CompilerParams(vmem_limit_bytes=GRANT)
    line_bytes = 4 * cells * lines
    source, fields, register = far(source), far(fields), far(register)
    metric_row, curvature_row = far(metric_row), far(curvature_row)
    semaphores = pltpu.SemaphoreType.DMA
    one_row = fast(1, cells)

    totals = pl.pallas_call(
        totals_kernel,
        in_specs=[hbm, hbm],
        out_specs=vmem,
        out_shape=fast(inner_count, groups, LANES),
        scratch_shapes=[fast(cells, lines), one_row, semaphores((3,))],
        compiler_params=params,
        cost_estimate=cost(line_bytes),
        name="totals",
    )(source, metric_row)
    inner_totals = lax.all_to_all(totals, "inner", 0, 0)

    lower = np.tril(np.ones((cells, cells))) - 0.5 * np.eye(cells)
    lower = jnp.asarray(np.concatenate([lower] * 3, axis=1), jnp.bfloat16)
    message_one, message_two, running, spread = pl.pallas_call(
        send_kernel,
        in_specs=[smem, hbm, hbm, hbm, hbm, hbm],
        out_specs=[vmem, vmem, vmem, vmem],
        out_shape=[fast(*message_shape(lines)), fast(*message_shape(lines)), fast(cells, lines), fast(cells, LANES)],
        scratch_shapes=[
            fast(3, cells, lines),
            fast(cells, lines),
            one_row,
            fast(cells, LANES),
            pltpu.VMEM((cells, 3 * cells), jnp.bfloat16),
            semaphores((3, 3)),
        ],
        compiler_params=params,
        cost_estimate=cost(4 * line_bytes),
        name="send",
    )(kind, fields, source, metric_row, far(jnp.asarray(send_weights)), far(lower))

    slab_sums = pl.pallas_call(
        slab_kernel,
        in_specs=[vmem, hbm, hbm],
        out_specs=vmem,
        out_shape=fast(slab_count, groups, LANES),
        compiler_params=params,
        name="slab",
    )(keep(inner_totals), message_one, message_two)
    slab_totals = lax.all_to_all(slab_sums, "slab", 0, 0)

    line = ("slab", "inner")
    even_pairs = [(i, i ^ 1) for i in range(count)]
    odd_pairs = [(i, i + 1 if i % 2 else i - 1) for i in range(1, count - 1)]
    got_two = lax.ppermute(message_two, line, odd_pairs)
    got_one = lax.ppermute(message_one, line, even_pairs)

    velocity, offset, rate = pl.pallas_call(
        velocity_kernel,
        in_specs=[smem, smem, vmem, vmem, vmem, vmem],
        out_specs=[vmem, vmem, vmem],
        out_shape=[fast(cells, lines), fast(1, lines), fast(devices, LANES)],
        compiler_params=params,
        cost_estimate=cost(2 * line_bytes),
        name="velocity",
    )(inner, slab, keep(running), keep(spread), keep(inner_totals), keep(slab_totals))

    rates = lax.all_to_all(rate, ("slab", "inner", "gz"), 0, 0, tiled=True)

    def half(*sizes):
        return pltpu.VMEM(sizes, jnp.bfloat16)

    edge = DEPTH - 3 * cells
    partial, held_fields, edge_mixed, edge_scalar, edge_drift, velocity_out = pl.pallas_call(
        inner_kernel,
        in_specs=[smem, hbm, hbm, vmem, vmem, hbm, hbm],
        out_specs=[vmem, vmem, vmem, vmem, vmem, hbm],
        out_shape=[
            fast(3, cells, lines),
            fast(3, cells, lines),
            half(2 * cells, edge),
            half(2 * cells, edge),
            half(cells, edge),
            pltpu.HBM((cells, lines), jnp.float32),
        ],
        scratch_shapes=[
            fast(cells, lines),
            fast(3, cells, DEPTH),
            one_row,
            half(2 * cells, DEPTH),
            half(2 * cells, DEPTH),
            half(cells, DEPTH),
            semaphores((3, 3)),
        ],
        compiler_params=params,
        cost_estimate=cost(12 * line_bytes),
        name="inner",
    )(kind, fields, source, keep(velocity), keep(spread), curvature_row, far(jnp.asarray(solve_tables)))

    tendency = pl.pallas_call(
        tendency_kernel,
        in_specs=[vmem] * 9,
        out_specs=vmem,
        out_shape=fast(3, cells, lines),
        compiler_params=params,
        cost_estimate=cost(8 * line_bytes),
        name="tendency",
    )(
        keep(partial), keep(held_fields), keep(velocity), keep(offset), keep(edge_mixed), keep(edge_scalar),
        keep(edge_drift), got_one, got_two,
    )

    new_fields, new_register = pl.pallas_call(
        update_kernel,
        in_specs=[hbm, hbm, vmem, vmem],
        out_specs=[hbm, hbm],
        out_shape=[pltpu.HBM((3, cells, lines), jnp.float32)] * 2,
        scratch_shapes=[fast(3, cells, lines), fast(3, cells, lines), semaphores((4, 3))],
        compiler_params=params,
        cost_estimate=cost(12 * line_bytes),
        name="update",
    )(fields, register, keep(tendency), rates)
    return (new_fields, new_register, velocity_out)


def solution(mesh):
    along, across = mesh.devices.shape
    inner = 1
    while inner * inner < along:
        inner *= 2
    split = Mesh(mesh.devices.reshape(along // inner, inner, across), ("slab", "inner", "gz"))
    line = ("slab", "inner")
    placed = (P(None, line, "gz"), P(None, line, "gz"), P(line, "gz"), P(line), P(line))
    return jax.shard_map(
        local,
        mesh=split,
        in_specs=placed,
        out_specs=(P(None, line, "gz"), P(None, line, "gz"), P(line, "gz")),
        check_vma=False,
    )
```

```python
import functools

import jax
import jax.numpy as jnp
import numpy as np
from jax import lax
from jax.experimental import pallas as pl
from jax.experimental.pallas import tpu as pltpu
from jax.sharding import Mesh
from jax.sharding import PartitionSpec as P

ALPHA_ONE = 1.0 / 3.0
COEF_ONE = 14.0 / 9.0
WIDE_ONE = 1.0 / 9.0
ALPHA_TWO = 2.0 / 11.0
COEF_TWO = 12.0 / 11.0
WIDE_TWO = 3.0 / 11.0
VISCOSITY = 0.25
DIFFUSIVITY = 0.2
COURANT = 1.2
KEEP_FACTOR = -5.0 / 9.0
STEP_FACTOR = 15.0 / 16.0

LANES = 128
SLAB_FIRST = 4
INNER_FIRST = 0
RATE_FIRST = (4, 2, 2)
STEPS = 4
GRANT = 24 * 1024 * 1024
MESSAGE = 11
DEPTH = 256


def inverse(alpha, length):
    matrix = np.eye(length) + alpha * (np.eye(length, k=1) + np.eye(length, k=-1))
    return np.linalg.inv(matrix)


@functools.cache
def operators(cells):
    length = 4 * cells
    near_up, near_down = np.eye(length, k=1), np.eye(length, k=-1)
    far_up, far_down = np.eye(length, k=2), np.eye(length, k=-2)
    first = COEF_ONE / 2.0 * (near_up - near_down) + WIDE_ONE / 4.0 * (far_up - far_down)
    second = COEF_TWO * (near_up - 2.0 * np.eye(length) + near_down) + WIDE_TWO / 4.0 * (
        far_up - 2.0 * np.eye(length) + far_down
    )
    slope = inverse(ALPHA_ONE, length) @ first
    bend = inverse(ALPHA_TWO, length) @ second
    integral = -(np.tril(np.ones((length, length))) - 0.5 * np.eye(length))
    constant = slope @ np.ones(length)
    return slope, bend, slope @ integral, constant


def from_left(matrix, block, cells):
    start = block * cells
    part = matrix[start : start + cells, start - cells : start]
    weights = part[1]
    factors = part[:, cells - 2] / part[1, cells - 2]
    corner = np.zeros(cells)
    corner[0] = part[0, cells - 1] - factors[0] * part[1, cells - 1]
    return factors, weights, corner


def from_right(matrix, block, cells):
    start = block * cells
    part = matrix[start : start + cells, start + cells : start + 2 * cells]
    weights = part[cells - 2]
    factors = part[:, 1] / part[cells - 2, 1]
    corner = np.zeros(cells)
    corner[cells - 1] = part[cells - 1, 0] - factors[cells - 1] * part[cells - 2, 0]
    return factors, weights, corner


@functools.cache
def tables(cells):
    slope, bend, drift, constant = operators(cells)
    kinds = (0, 2, 1, 3)
    send = np.zeros((4, cells, LANES))
    solve = np.zeros((4, 3, cells, DEPTH))
    for kind, block in enumerate(kinds):
        odd = kind >= 2
        start = block * cells
        own = slice(start, start + cells)
        rest = np.zeros(4 * cells)
        if block == 3:
            rest[own] = constant[own]
        local = drift + rest[:, None] * (np.arange(4 * cells) < start)[None, :]
        for which, matrix in enumerate((slope, bend, local)):
            base = np.zeros((cells, cells + 8))
            base[:, :cells] = matrix[own, own]
            left, right = (0, 4) if odd else (4, 0)
            slot = 1 if which == 1 else 0
            if block > 0:
                factors, _, corner = from_left(matrix, block, cells)
                base[:, cells + left + slot] = factors
                base[:, cells + left + 2] = corner
            if block < 3:
                factors, _, corner = from_right(matrix, block, cells)
                base[:, cells + right + slot] = factors
                base[:, cells + right + 2] = corner
            if which == 2:
                base[:, cells + 1] = -rest[own]
            for copy in range(3):
                solve[kind, which, :, copy * cells : (copy + 1) * cells] = base[:, :cells]
                solve[kind, which, :, 3 * cells + 8 * copy : 3 * cells + 8 * copy + 8] = base[:, cells:]
            to_right = to_left = np.zeros(cells)
            sent = (slope, bend, drift)[which]
            if block < 2:
                to_right = from_left(sent, block + 1, cells)[1]
            elif block == 2:
                to_right = from_left(sent, 2, cells)[1]
            if block > 0:
                to_left = from_right(sent, block - 1, cells)[1]
            pair = (to_left, to_right) if odd else (to_right, to_left)
            send[kind, :, which] = pair[0]
            send[kind, :, 3 + which] = pair[1]
    return send.astype(np.float32), solve.astype(np.float32)


def column(row):
    size = row.shape[1]
    rows = lax.broadcasted_iota(jnp.int32, (size, size), 0)
    columns = lax.broadcasted_iota(jnp.int32, (size, size), 1)
    spread = jnp.broadcast_to(row, (size, size))
    return jnp.sum(jnp.where(rows == columns, spread, 0.0), axis=1, keepdims=True)


def halves(value):
    high = value.astype(jnp.bfloat16)
    low = (value - high.astype(jnp.float32)).astype(jnp.bfloat16)
    return high, low


def pieces_of(lines, count=STEPS):
    width = lines // count
    return [slice(start, start + width) for start in range(0, lines, width)]


def message_shape(lines):
    return 8, lines + (MESSAGE - 8) * (lines // 8)


def put(message, row, part, value):
    width = value.shape[1]
    fold = width // 2
    if row < 8:
        message[row : row + 1, part * width : (part + 1) * width] = value
        return
    start = STEPS * width + (row - 8) * fold
    for half in range(2):
        line = 2 * part + half
        message[line : line + 1, start : start + fold] = value[:, half * fold : (half + 1) * fold]


def take(message, row, part, width):
    fold = width // 2
    if row < 8:
        return message[row : row + 1, part * width : (part + 1) * width]
    start = STEPS * width + (row - 8) * fold
    return jnp.concatenate(
        [message[2 * part + half : 2 * part + half + 1, start : start + fold] for half in range(2)], axis=1
    )


def totals_kernel(source, metric, totals, held, held_metric, sems):
    cells, lines = source.shape
    metric_copy = pltpu.make_async_copy(metric, held_metric, sems.at[2])
    metric_copy.start()
    rows = [slice(0, cells // 2), slice(cells // 2, cells)]
    copies = [pltpu.make_async_copy(source.at[r, :], held.at[r, :], sems.at[i]) for i, r in enumerate(rows)]
    for copy in copies:
        copy.start()
    metric_copy.wait()
    scale = 1.0 / column(held_metric[...])
    total = jnp.zeros((1, lines), jnp.float32)
    for copy, r in zip(copies, rows):
        copy.wait()
        total += jnp.sum(held[r, :] * scale[r], axis=0, keepdims=True)
    for peer in range(totals.shape[0]):
        for k in range(lines // LANES):
            totals[peer, k : k + 1, :] = total[:, k * LANES : (k + 1) * LANES]


def send_kernel(
    kind, fields, source, metric, weights, lower, message_one, message_two, running, spread,
    held, held_source, held_metric, held_weights, held_lower, sems,
):
    cells, lines = source.shape
    pieces = pieces_of(lines, STEPS // 2)
    metric_copy = pltpu.make_async_copy(metric, held_metric, sems.at[2, 0])
    metric_copy.start()
    weights_copy = pltpu.make_async_copy(weights.at[kind[0]], held_weights, sems.at[2, 1])
    weights_copy.start()
    lower_copy = pltpu.make_async_copy(lower, held_lower, sems.at[2, 2])
    lower_copy.start()
    copies = []
    for i, p in enumerate(pieces):
        pair = (
            pltpu.make_async_copy(source.at[:, p], held_source.at[:, p], sems.at[1, i]),
            pltpu.make_async_copy(fields.at[:, :, p], held.at[:, :, p], sems.at[0, i]),
        )
        for copy in pair:
            copy.start()
        copies.append(pair)
    odd = kind[0] >= 2
    metric_copy.wait()
    weights_copy.wait()
    lower_copy.wait()
    chosen = held_weights[...]
    stretch = column(held_metric[...])
    spread[...] = jnp.broadcast_to(stretch, spread.shape)
    scale = 1.0 / stretch
    for i, p in enumerate(pieces_of(lines)):
        if i % 2 == 0:
            for copy in copies[i // 2]:
                copy.wait()
        scaled = held_source[:, p] * scale
        high = scaled.astype(jnp.bfloat16)
        rest = scaled - high.astype(jnp.float32)
        middle = rest.astype(jnp.bfloat16)
        low = (rest - middle.astype(jnp.float32)).astype(jnp.bfloat16)
        running[:, p] = jnp.dot(
            held_lower[...], jnp.concatenate([high, middle, low], axis=0), preferred_element_type=jnp.float32
        )
        for k in range(4):
            value = held[k, :, p] if k < 3 else scaled
            first, last = value[:1], value[cells - 1 :]
            for message, begin in ((message_one, 0), (message_two, 3)):
                row = 3 * k
                for which in range(2) if k < 3 else (2,):
                    weight = chosen[:, begin + which : begin + which + 1]
                    put(message, row, i, jnp.sum(value * weight, axis=0, keepdims=True))
                    row += 1
                put(message, row, i, jnp.where(odd, first, last) if begin == 0 else jnp.where(odd, last, first))


def slab_kernel(inner, after_one, after_two, sums):
    del after_one, after_two
    total = inner[0]
    for peer in range(1, inner.shape[0]):
        total += inner[peer]
    for peer in range(sums.shape[0]):
        sums[peer] = total


def velocity_kernel(place, slab, running, spread, inner, outer, velocity, offset, rate):
    stretch = spread[...]
    squared = 4.0 * VISCOSITY * stretch * stretch
    before = jnp.zeros(inner.shape[1:], jnp.float32)
    for peer in range(inner.shape[0]):
        owner = (peer + INNER_FIRST) % inner.shape[0]
        before += jnp.where(owner < place[0], inner[peer], 0.0)
    for peer in range(outer.shape[0]):
        owner = (peer + SLAB_FIRST) % outer.shape[0]
        before += jnp.where(owner < slab[0], outer[peer], 0.0)
    top = jnp.zeros((1, LANES), jnp.float32)
    for k in range(before.shape[0]):
        here = slice(k * LANES, (k + 1) * LANES)
        shift = before[k : k + 1, :]
        offset[:, here] = shift
        value = -(running[:, here] + shift)
        velocity[:, here] = value
        top = jnp.maximum(top, jnp.max(jnp.abs(value) * stretch + squared, axis=0, keepdims=True))
    peak = jnp.max(top, axis=1, keepdims=True)
    rate[...] = jnp.broadcast_to(peak, rate.shape)


def tendency_kernel(
    kind, fields, source, velocity, offset, spread, message_one, message_two, curvature, table,
    tendency, velocity_out,
    held_fields, held_source, held_table, held_curvature, mixed, mixed_scalar, drift, sems,
):
    cells, lines = source.shape
    pieces = pieces_of(lines, STEPS // 2)
    table_copy = pltpu.make_async_copy(table.at[kind[0]], held_table, sems.at[2, 0])
    table_copy.start()
    curvature_copy = pltpu.make_async_copy(curvature, held_curvature, sems.at[2, 1])
    curvature_copy.start()
    copies = []
    for i, p in enumerate(pieces):
        group = (
            pltpu.make_async_copy(source.at[:, p], held_source.at[:, p], sems.at[0, i]),
            pltpu.make_async_copy(fields.at[:, :, p], held_fields.at[:, :, p], sems.at[1, i]),
        )
        for copy in group:
            copy.start()
        copies.append(group)
    out_copy = pltpu.make_async_copy(velocity, velocity_out, sems.at[2, 2])
    out_copy.start()

    stretch = spread[:, :1]
    table_copy.wait()
    curvature_copy.wait()
    curving = column(held_curvature[...])
    slope, bend = held_table[0], held_table[1]
    lane = lax.broadcasted_iota(jnp.int32, (cells, DEPTH), 1)
    is_low = ((lane >= 2 * cells) & (lane < 3 * cells)) | (lane >= 3 * cells + 16)

    def split(value):
        high, low = halves(value)
        return jnp.where(is_low, low.astype(jnp.float32), high.astype(jnp.float32)).astype(jnp.bfloat16)

    field_x = stretch * slope
    field_xx = stretch * stretch * bend + curving * slope
    mixed[:cells, :] = split(field_x)
    mixed[cells:, :] = split(VISCOSITY * field_xx)
    mixed_scalar[:cells, :] = mixed[:cells, :]
    mixed_scalar[cells:, :] = split(DIFFUSIVITY * field_xx)
    drift[...] = split(stretch * held_table[2])

    def stacked(value, tail):
        high, low = halves(value)
        tail_high = tail.astype(jnp.bfloat16).astype(jnp.float32)
        tail_low = tail - tail_high
        tails = jnp.concatenate(
            [tail_high, tail_low, tail_high, jnp.zeros((DEPTH - 3 * cells - 24, width), jnp.float32)], axis=0
        ).astype(jnp.bfloat16)
        return jnp.concatenate([high, low, high, tails], axis=0)

    width = lines // STEPS
    blank = jnp.zeros((1, width), jnp.float32)

    def tails(rows, part, second):
        found = [[blank if row is None else take(message, row, part, width) for row in rows] for message in (message_one, message_two)]
        return jnp.concatenate([found[0][0], found[0][1] if second is None else second, *found[0][2:], *found[1]], axis=0)

    for i, p in enumerate(pieces_of(lines)):
        if i % 2 == 0:
            copies[i // 2][0].wait()
        scaled = held_source[:, p] * (1.0 / stretch)
        tail = tails((9, None, 10, None), i, offset[:, p])
        velocity_x = jnp.dot(drift[...], stacked(scaled, tail), preferred_element_type=jnp.float32)
        speed = velocity[:, p]
        if i % 2 == 0:
            copies[i // 2][1].wait()
        for k in range(3):
            field = held_fields[k, :, p]
            tail = tails((3 * k, 3 * k + 1, 3 * k + 2, None), i, None)
            weights = mixed if k < 2 else mixed_scalar
            both = jnp.dot(weights[...], stacked(field, tail), preferred_element_type=jnp.float32)
            tendency[k, :, p] = both[cells:] - (speed * both[:cells] + field * velocity_x)
    out_copy.wait()


def update_kernel(fields, register, tendency, rates, more_rates, new_fields, new_register, held_fields, held_register, sems):
    cells = tendency.shape[1]
    edges = [0, 3 * cells // 8, 3 * cells // 4, cells]
    pieces = [(slice(None), slice(low, high)) for low, high in zip(edges[:-1], edges[1:])]
    arrivals = []
    for i, p in enumerate(pieces):
        pair = (
            pltpu.make_async_copy(register.at[p], held_register.at[p], sems.at[0, i]),
            pltpu.make_async_copy(fields.at[p], held_fields.at[p], sems.at[1, i]),
        )
        for copy in pair:
            copy.start()
        arrivals.append(pair)
    highest = jnp.maximum(rates[...], more_rates[...])
    time_step = COURANT / jnp.max(jnp.max(highest, axis=0, keepdims=True), axis=1, keepdims=True)
    departures = []
    for i, p in enumerate(pieces):
        arrivals[i][0].wait()
        updated = KEEP_FACTOR * held_register[p] + time_step * tendency[p]
        held_register[p] = updated
        departures.append(pltpu.make_async_copy(held_register.at[p], new_register.at[p], sems.at[2, i]))
        departures[-1].start()
        arrivals[i][1].wait()
        held_fields[p] = held_fields[p] + STEP_FACTOR * updated
        departures.append(pltpu.make_async_copy(held_fields.at[p], new_fields.at[p], sems.at[3, i]))
        departures[-1].start()
    for copy in departures:
        copy.wait()


def turned(first, count):
    return [[(i + first) % count for i in range(count)]]


def local(fields, register, source, metric, curvature):
    cells, lines = source.shape
    groups = lines // LANES
    near, line, same_core = ("ring", "core"), ("slab", "ring", "core"), ("slab", "ring", "gz")
    inner_count, slab_count = lax.axis_size(near), lax.axis_size("slab")
    count = inner_count * slab_count
    devices = lax.axis_size(same_core)
    inner, slab = lax.axis_index(near), lax.axis_index("slab")
    position = slab * inner_count + inner
    kind = jnp.where(position == 0, 0, jnp.where(position == count - 1, 3, 1 + position % 2))
    kind, inner, slab = (jnp.reshape(value, (1,)).astype(jnp.int32) for value in (kind, inner, slab))
    send_weights, solve_tables = tables(cells)
    metric_row, curvature_row = metric[None, :], curvature[None, :]

    smem = pl.BlockSpec(memory_space=pltpu.SMEM)
    vmem = pl.BlockSpec(memory_space=pltpu.VMEM)
    hbm = pl.BlockSpec(memory_space=pl.ANY)

    def shape(*sizes):
        return jax.ShapeDtypeStruct(sizes, jnp.float32)

    def fast(*sizes):
        return pltpu.VMEM(sizes, jnp.float32)

    def keep(value):
        return pltpu.with_memory_space_constraint(value, pltpu.VMEM)

    def far(value):
        return pltpu.with_memory_space_constraint(value, pltpu.HBM)

    def cost(bytes_accessed, flops=0):
        return pl.CostEstimate(flops=flops, bytes_accessed=bytes_accessed, transcendentals=0)

    params = pltpu.CompilerParams(vmem_limit_bytes=GRANT)
    line_bytes = 4 * cells * lines
    source, fields, register = far(source), far(fields), far(register)
    metric_row, curvature_row = far(metric_row), far(curvature_row)
    semaphores = pltpu.SemaphoreType.DMA
    one_row = fast(1, cells)

    totals = pl.pallas_call(
        totals_kernel,
        in_specs=[hbm, hbm],
        out_specs=vmem,
        out_shape=fast(inner_count, groups, LANES),
        scratch_shapes=[fast(cells, lines), one_row, semaphores((3,))],
        compiler_params=params,
        cost_estimate=cost(line_bytes),
        name="totals",
    )(source, metric_row)
    inner_totals = lax.all_to_all(totals, near, 0, 0, axis_index_groups=turned(INNER_FIRST, inner_count))

    lower = np.tril(np.ones((cells, cells))) - 0.5 * np.eye(cells)
    lower = jnp.asarray(np.concatenate([lower] * 3, axis=1), jnp.bfloat16)
    message_one, message_two, running, spread = pl.pallas_call(
        send_kernel,
        in_specs=[smem, hbm, hbm, hbm, hbm, hbm],
        out_specs=[vmem, vmem, vmem, vmem],
        out_shape=[fast(*message_shape(lines)), fast(*message_shape(lines)), fast(cells, lines), fast(cells, LANES)],
        scratch_shapes=[
            fast(3, cells, lines),
            fast(cells, lines),
            one_row,
            fast(cells, LANES),
            pltpu.VMEM((cells, 3 * cells), jnp.bfloat16),
            semaphores((3, 3)),
        ],
        compiler_params=params,
        cost_estimate=cost(4 * line_bytes),
        name="send",
    )(kind, fields, source, metric_row, far(jnp.asarray(send_weights)), far(lower))

    slab_sums = pl.pallas_call(
        slab_kernel,
        in_specs=[vmem, hbm, hbm],
        out_specs=vmem,
        out_shape=fast(slab_count, groups, LANES),
        compiler_params=params,
        name="slab",
    )(keep(inner_totals), message_one, message_two)
    slab_totals = lax.all_to_all(slab_sums, "slab", 0, 0, axis_index_groups=turned(SLAB_FIRST, slab_count))

    even_pairs = [(i, i ^ 1) for i in range(count)]
    odd_pairs = [(i, i + 1 if i % 2 else i - 1) for i in range(1, count - 1)]
    got_two = lax.ppermute(message_two, line, odd_pairs)
    got_one = lax.ppermute(message_one, line, even_pairs)

    velocity, offset, rate = pl.pallas_call(
        velocity_kernel,
        in_specs=[smem, smem, vmem, vmem, vmem, vmem],
        out_specs=[vmem, vmem, vmem],
        out_shape=[fast(cells, lines), fast(1, lines), fast(devices, LANES)],
        compiler_params=params,
        cost_estimate=cost(2 * line_bytes),
        name="velocity",
    )(inner, slab, keep(running), keep(spread), keep(inner_totals), keep(slab_totals))

    order = np.arange(devices).reshape([lax.axis_size(axis) for axis in same_core])
    order = [int(i) for i in np.roll(order, [-turn for turn in RATE_FIRST], axis=(0, 1, 2)).ravel()]
    rates = lax.all_to_all(rate, same_core, 0, 0, axis_index_groups=[order], tiled=True)

    tendency, velocity_out = pl.pallas_call(
        tendency_kernel,
        in_specs=[smem, hbm, hbm, vmem, vmem, vmem, vmem, vmem, hbm, hbm],
        out_specs=[vmem, hbm],
        out_shape=[fast(3, cells, lines), pltpu.HBM((cells, lines), jnp.float32)],
        scratch_shapes=[
            fast(3, cells, lines),
            fast(cells, lines),
            fast(3, cells, DEPTH),
            one_row,
            pltpu.VMEM((2 * cells, DEPTH), jnp.bfloat16),
            pltpu.VMEM((2 * cells, DEPTH), jnp.bfloat16),
            pltpu.VMEM((cells, DEPTH), jnp.bfloat16),
            semaphores((3, 3)),
        ],
        compiler_params=params,
        cost_estimate=cost(12 * line_bytes),
        name="tendency",
    )(
        kind, fields, source, keep(velocity), keep(offset), keep(spread), got_one, got_two, curvature_row,
        far(jnp.asarray(solve_tables)),
    )

    rates, tendency = lax.optimization_barrier((rates, tendency))
    more_rates = lax.ppermute(rates, "core", [(0, 1), (1, 0)])
    new_fields, new_register = pl.pallas_call(
        update_kernel,
        in_specs=[hbm, hbm, vmem, vmem, vmem],
        out_specs=[hbm, hbm],
        out_shape=[pltpu.HBM((3, cells, lines), jnp.float32)] * 2,
        scratch_shapes=[fast(3, cells, lines), fast(3, cells, lines), semaphores((4, 3))],
        compiler_params=params,
        cost_estimate=cost(12 * line_bytes),
        name="update",
    )(fields, register, keep(tendency), keep(rates), keep(more_rates))
    return (new_fields, new_register, velocity_out)


def solution(mesh):
    along, across = mesh.devices.shape
    inner = 1
    while inner * inner < along:
        inner *= 2
    shape = (along // inner, inner // 2, 2, across)
    split = Mesh(mesh.devices.reshape(shape), ("slab", "ring", "core", "gz"))
    line = ("slab", "ring", "core")
    placed = (P(None, line, "gz"), P(None, line, "gz"), P(line, "gz"), P(line), P(line))
    return jax.shard_map(
        local,
        mesh=split,
        in_specs=placed,
        out_specs=(P(None, line, "gz"), P(None, line, "gz"), P(line, "gz")),
        check_vma=False,
    )
```

```python
import functools

import jax
import jax.numpy as jnp
import numpy as np
from jax import lax
from jax.experimental import pallas as pl
from jax.experimental.pallas import tpu as pltpu
from jax.sharding import Mesh
from jax.sharding import PartitionSpec as P

ALPHA_ONE = 1.0 / 3.0
COEF_ONE = 14.0 / 9.0
WIDE_ONE = 1.0 / 9.0
ALPHA_TWO = 2.0 / 11.0
COEF_TWO = 12.0 / 11.0
WIDE_TWO = 3.0 / 11.0
VISCOSITY = 0.25
DIFFUSIVITY = 0.2
COURANT = 1.2
KEEP_FACTOR = -5.0 / 9.0
STEP_FACTOR = 15.0 / 16.0

LANES = 128
SLAB_FIRST = 4
INNER_FIRST = 0
RATE_FIRST = (4, 1, 2)
STEPS = 4
GRANT = 24 * 1024 * 1024
MESSAGE = 11
DEPTH = 256


def inverse(alpha, length):
    matrix = np.eye(length) + alpha * (np.eye(length, k=1) + np.eye(length, k=-1))
    return np.linalg.inv(matrix)


@functools.cache
def operators(cells):
    length = 4 * cells
    near_up, near_down = np.eye(length, k=1), np.eye(length, k=-1)
    far_up, far_down = np.eye(length, k=2), np.eye(length, k=-2)
    first = COEF_ONE / 2.0 * (near_up - near_down) + WIDE_ONE / 4.0 * (far_up - far_down)
    second = COEF_TWO * (near_up - 2.0 * np.eye(length) + near_down) + WIDE_TWO / 4.0 * (
        far_up - 2.0 * np.eye(length) + far_down
    )
    slope = inverse(ALPHA_ONE, length) @ first
    bend = inverse(ALPHA_TWO, length) @ second
    integral = -(np.tril(np.ones((length, length))) - 0.5 * np.eye(length))
    constant = slope @ np.ones(length)
    return slope, bend, slope @ integral, constant


def from_left(matrix, block, cells):
    start = block * cells
    part = matrix[start : start + cells, start - cells : start]
    weights = part[1]
    factors = part[:, cells - 2] / part[1, cells - 2]
    corner = np.zeros(cells)
    corner[0] = part[0, cells - 1] - factors[0] * part[1, cells - 1]
    return factors, weights, corner


def from_right(matrix, block, cells):
    start = block * cells
    part = matrix[start : start + cells, start + cells : start + 2 * cells]
    weights = part[cells - 2]
    factors = part[:, 1] / part[cells - 2, 1]
    corner = np.zeros(cells)
    corner[cells - 1] = part[cells - 1, 0] - factors[cells - 1] * part[cells - 2, 0]
    return factors, weights, corner


@functools.cache
def tables(cells):
    slope, bend, drift, constant = operators(cells)
    kinds = (0, 2, 1, 3)
    send = np.zeros((4, cells, LANES))
    solve = np.zeros((4, 3, cells, DEPTH))
    for kind, block in enumerate(kinds):
        odd = kind >= 2
        start = block * cells
        own = slice(start, start + cells)
        rest = np.zeros(4 * cells)
        if block == 3:
            rest[own] = constant[own]
        local = drift + rest[:, None] * (np.arange(4 * cells) < start)[None, :]
        for which, matrix in enumerate((slope, bend, local)):
            base = np.zeros((cells, cells + 8))
            base[:, :cells] = matrix[own, own]
            left, right = (0, 4) if odd else (4, 0)
            slot = 1 if which == 1 else 0
            if block > 0:
                factors, _, corner = from_left(matrix, block, cells)
                base[:, cells + left + slot] = factors
                base[:, cells + left + 2] = corner
            if block < 3:
                factors, _, corner = from_right(matrix, block, cells)
                base[:, cells + right + slot] = factors
                base[:, cells + right + 2] = corner
            if which == 2:
                base[:, cells + 1] = -rest[own]
            for copy in range(3):
                solve[kind, which, :, copy * cells : (copy + 1) * cells] = base[:, :cells]
                solve[kind, which, :, 3 * cells + 8 * copy : 3 * cells + 8 * copy + 8] = base[:, cells:]
            to_right = to_left = np.zeros(cells)
            sent = (slope, bend, drift)[which]
            if block < 2:
                to_right = from_left(sent, block + 1, cells)[1]
            elif block == 2:
                to_right = from_left(sent, 2, cells)[1]
            if block > 0:
                to_left = from_right(sent, block - 1, cells)[1]
            pair = (to_left, to_right) if odd else (to_right, to_left)
            send[kind, :, which] = pair[0]
            send[kind, :, 3 + which] = pair[1]
    return send.astype(np.float32), solve.astype(np.float32)


def column(row):
    size = row.shape[1]
    rows = lax.broadcasted_iota(jnp.int32, (size, size), 0)
    columns = lax.broadcasted_iota(jnp.int32, (size, size), 1)
    spread = jnp.broadcast_to(row, (size, size))
    return jnp.sum(jnp.where(rows == columns, spread, 0.0), axis=1, keepdims=True)


def halves(value):
    high = value.astype(jnp.bfloat16)
    low = (value - high.astype(jnp.float32)).astype(jnp.bfloat16)
    return high, low


def pieces_of(lines, count=STEPS):
    width = lines // count
    return [slice(start, start + width) for start in range(0, lines, width)]


def message_shape(lines):
    return 8, lines + (MESSAGE - 8) * (lines // 8)


def put(message, row, part, value):
    width = value.shape[1]
    fold = width // 2
    if row < 8:
        message[row : row + 1, part * width : (part + 1) * width] = value
        return
    start = STEPS * width + (row - 8) * fold
    for half in range(2):
        line = 2 * part + half
        message[line : line + 1, start : start + fold] = value[:, half * fold : (half + 1) * fold]


def take(message, row, part, width):
    fold = width // 2
    if row < 8:
        return message[row : row + 1, part * width : (part + 1) * width]
    start = STEPS * width + (row - 8) * fold
    return jnp.concatenate(
        [message[2 * part + half : 2 * part + half + 1, start : start + fold] for half in range(2)], axis=1
    )


def totals_kernel(source, metric, totals, held, held_metric, sems):
    cells, lines = source.shape
    metric_copy = pltpu.make_async_copy(metric, held_metric, sems.at[2])
    metric_copy.start()
    rows = [slice(0, cells // 2), slice(cells // 2, cells)]
    copies = [pltpu.make_async_copy(source.at[r, :], held.at[r, :], sems.at[i]) for i, r in enumerate(rows)]
    for copy in copies:
        copy.start()
    metric_copy.wait()
    scale = 1.0 / column(held_metric[...])
    total = jnp.zeros((1, lines), jnp.float32)
    for copy, r in zip(copies, rows):
        copy.wait()
        total += jnp.sum(held[r, :] * scale[r], axis=0, keepdims=True)
    for peer in range(totals.shape[0]):
        for k in range(lines // LANES):
            totals[peer, k : k + 1, :] = total[:, k * LANES : (k + 1) * LANES]


def send_kernel(
    kind, fields, source, metric, weights, lower, message_one, message_two, running, spread,
    held, held_source, held_metric, held_weights, held_lower, sems,
):
    cells, lines = source.shape
    pieces = pieces_of(lines, STEPS // 2)
    metric_copy = pltpu.make_async_copy(metric, held_metric, sems.at[2, 0])
    metric_copy.start()
    weights_copy = pltpu.make_async_copy(weights.at[kind[0]], held_weights, sems.at[2, 1])
    weights_copy.start()
    lower_copy = pltpu.make_async_copy(lower, held_lower, sems.at[2, 2])
    lower_copy.start()
    copies = []
    for i, p in enumerate(pieces):
        pair = (
            pltpu.make_async_copy(source.at[:, p], held_source.at[:, p], sems.at[1, i]),
            pltpu.make_async_copy(fields.at[:, :, p], held.at[:, :, p], sems.at[0, i]),
        )
        for copy in pair:
            copy.start()
        copies.append(pair)
    odd = kind[0] >= 2
    metric_copy.wait()
    weights_copy.wait()
    lower_copy.wait()
    chosen = held_weights[...]
    stretch = column(held_metric[...])
    spread[...] = jnp.broadcast_to(stretch, spread.shape)
    scale = 1.0 / stretch
    for i, p in enumerate(pieces_of(lines)):
        if i % 2 == 0:
            for copy in copies[i // 2]:
                copy.wait()
        scaled = held_source[:, p] * scale
        high = scaled.astype(jnp.bfloat16)
        rest = scaled - high.astype(jnp.float32)
        middle = rest.astype(jnp.bfloat16)
        low = (rest - middle.astype(jnp.float32)).astype(jnp.bfloat16)
        running[:, p] = jnp.dot(
            held_lower[...], jnp.concatenate([high, middle, low], axis=0), preferred_element_type=jnp.float32
        )
        for k in range(4):
            value = held[k, :, p] if k < 3 else scaled
            first, last = value[:1], value[cells - 1 :]
            for message, begin in ((message_one, 0), (message_two, 3)):
                row = 3 * k
                for which in range(2) if k < 3 else (2,):
                    weight = chosen[:, begin + which : begin + which + 1]
                    put(message, row, i, jnp.sum(value * weight, axis=0, keepdims=True))
                    row += 1
                put(message, row, i, jnp.where(odd, first, last) if begin == 0 else jnp.where(odd, last, first))


def slab_kernel(inner, after_one, after_two, sums):
    del after_one, after_two
    total = inner[0]
    for peer in range(1, inner.shape[0]):
        total += inner[peer]
    for peer in range(sums.shape[0]):
        sums[peer] = total


def velocity_kernel(place, slab, running, spread, inner, outer, velocity, offset, rate):
    stretch = spread[...]
    squared = 4.0 * VISCOSITY * stretch * stretch
    before = jnp.zeros(inner.shape[1:], jnp.float32)
    for peer in range(inner.shape[0]):
        owner = (peer + INNER_FIRST) % inner.shape[0]
        before += jnp.where(owner < place[0], inner[peer], 0.0)
    for peer in range(outer.shape[0]):
        owner = (peer + SLAB_FIRST) % outer.shape[0]
        before += jnp.where(owner < slab[0], outer[peer], 0.0)
    top = jnp.zeros((1, LANES), jnp.float32)
    for k in range(before.shape[0]):
        here = slice(k * LANES, (k + 1) * LANES)
        shift = before[k : k + 1, :]
        offset[:, here] = shift
        value = -(running[:, here] + shift)
        velocity[:, here] = value
        top = jnp.maximum(top, jnp.max(jnp.abs(value) * stretch + squared, axis=0, keepdims=True))
    peak = jnp.max(top, axis=1, keepdims=True)
    rate[...] = jnp.broadcast_to(peak, rate.shape)


def tendency_kernel(
    kind, fields, source, velocity, offset, spread, message_one, message_two, curvature, table,
    tendency, velocity_out,
    held_fields, held_source, held_table, held_curvature, mixed, mixed_scalar, drift, sems,
):
    cells, lines = source.shape
    pieces = pieces_of(lines, STEPS // 2)
    table_copy = pltpu.make_async_copy(table.at[kind[0]], held_table, sems.at[2, 0])
    table_copy.start()
    curvature_copy = pltpu.make_async_copy(curvature, held_curvature, sems.at[2, 1])
    curvature_copy.start()
    copies = []
    for i, p in enumerate(pieces):
        group = (
            pltpu.make_async_copy(source.at[:, p], held_source.at[:, p], sems.at[0, i]),
            pltpu.make_async_copy(fields.at[:, :, p], held_fields.at[:, :, p], sems.at[1, i]),
        )
        for copy in group:
            copy.start()
        copies.append(group)
    out_copy = pltpu.make_async_copy(velocity, velocity_out, sems.at[2, 2])
    out_copy.start()

    stretch = spread[:, :1]
    table_copy.wait()
    curvature_copy.wait()
    curving = column(held_curvature[...])
    slope, bend = held_table[0], held_table[1]
    lane = lax.broadcasted_iota(jnp.int32, (cells, DEPTH), 1)
    is_low = ((lane >= 2 * cells) & (lane < 3 * cells)) | (lane >= 3 * cells + 16)

    def split(value):
        high, low = halves(value)
        return jnp.where(is_low, low.astype(jnp.float32), high.astype(jnp.float32)).astype(jnp.bfloat16)

    field_x = stretch * slope
    field_xx = stretch * stretch * bend + curving * slope
    mixed[:cells, :] = split(field_x)
    mixed[cells:, :] = split(VISCOSITY * field_xx)
    mixed_scalar[:cells, :] = mixed[:cells, :]
    mixed_scalar[cells:, :] = split(DIFFUSIVITY * field_xx)
    drift[...] = split(stretch * held_table[2])

    def stacked(value, tail):
        high, low = halves(value)
        tail_high = tail.astype(jnp.bfloat16).astype(jnp.float32)
        tail_low = tail - tail_high
        tails = jnp.concatenate(
            [tail_high, tail_low, tail_high, jnp.zeros((DEPTH - 3 * cells - 24, width), jnp.float32)], axis=0
        ).astype(jnp.bfloat16)
        return jnp.concatenate([high, low, high, tails], axis=0)

    width = lines // STEPS
    blank = jnp.zeros((1, width), jnp.float32)

    def tails(rows, part, second):
        found = [[blank if row is None else take(message, row, part, width) for row in rows] for message in (message_one, message_two)]
        return jnp.concatenate([found[0][0], found[0][1] if second is None else second, *found[0][2:], *found[1]], axis=0)

    for i, p in enumerate(pieces_of(lines)):
        if i % 2 == 0:
            copies[i // 2][0].wait()
        scaled = held_source[:, p] * (1.0 / stretch)
        tail = tails((9, None, 10, None), i, offset[:, p])
        velocity_x = jnp.dot(drift[...], stacked(scaled, tail), preferred_element_type=jnp.float32)
        speed = velocity[:, p]
        if i % 2 == 0:
            copies[i // 2][1].wait()
        for k in range(3):
            field = held_fields[k, :, p]
            tail = tails((3 * k, 3 * k + 1, 3 * k + 2, None), i, None)
            weights = mixed if k < 2 else mixed_scalar
            both = jnp.dot(weights[...], stacked(field, tail), preferred_element_type=jnp.float32)
            tendency[k, :, p] = both[cells:] - (speed * both[:cells] + field * velocity_x)
    out_copy.wait()


def update_kernel(fields, register, tendency, rates, more_rates, new_fields, new_register, held_fields, held_register, sems):
    cells = tendency.shape[1]
    edges = [0, 3 * cells // 8, 3 * cells // 4, cells]
    pieces = [(slice(None), slice(low, high)) for low, high in zip(edges[:-1], edges[1:])]
    arrivals = []
    for i, p in enumerate(pieces):
        pair = (
            pltpu.make_async_copy(register.at[p], held_register.at[p], sems.at[0, i]),
            pltpu.make_async_copy(fields.at[p], held_fields.at[p], sems.at[1, i]),
        )
        for copy in pair:
            copy.start()
        arrivals.append(pair)
    highest = jnp.maximum(rates[...], more_rates[...])
    time_step = COURANT / jnp.max(jnp.max(highest, axis=0, keepdims=True), axis=1, keepdims=True)
    departures = []
    for i, p in enumerate(pieces):
        arrivals[i][0].wait()
        updated = KEEP_FACTOR * held_register[p] + time_step * tendency[p]
        held_register[p] = updated
        departures.append(pltpu.make_async_copy(held_register.at[p], new_register.at[p], sems.at[2, i]))
        departures[-1].start()
        arrivals[i][1].wait()
        held_fields[p] = held_fields[p] + STEP_FACTOR * updated
        departures.append(pltpu.make_async_copy(held_fields.at[p], new_fields.at[p], sems.at[3, i]))
        departures[-1].start()
    for copy in departures:
        copy.wait()


def turned(first, count):
    return [[(i + first) % count for i in range(count)]]


def local(fields, register, source, metric, curvature):
    cells, lines = source.shape
    groups = lines // LANES
    near, line, same_core = ("ring", "core"), ("slab", "ring", "core"), ("slab", "ring", "gz")
    inner_count, slab_count = lax.axis_size(near), lax.axis_size("slab")
    count = inner_count * slab_count
    devices = lax.axis_size(same_core)
    inner, slab = lax.axis_index(near), lax.axis_index("slab")
    position = slab * inner_count + inner
    kind = jnp.where(position == 0, 0, jnp.where(position == count - 1, 3, 1 + position % 2))
    kind, inner, slab = (jnp.reshape(value, (1,)).astype(jnp.int32) for value in (kind, inner, slab))
    send_weights, solve_tables = tables(cells)
    metric_row, curvature_row = metric[None, :], curvature[None, :]

    smem = pl.BlockSpec(memory_space=pltpu.SMEM)
    vmem = pl.BlockSpec(memory_space=pltpu.VMEM)
    hbm = pl.BlockSpec(memory_space=pl.ANY)

    def shape(*sizes):
        return jax.ShapeDtypeStruct(sizes, jnp.float32)

    def fast(*sizes):
        return pltpu.VMEM(sizes, jnp.float32)

    def keep(value):
        return pltpu.with_memory_space_constraint(value, pltpu.VMEM)

    def far(value):
        return pltpu.with_memory_space_constraint(value, pltpu.HBM)

    def cost(bytes_accessed, flops=0):
        return pl.CostEstimate(flops=flops, bytes_accessed=bytes_accessed, transcendentals=0)

    params = pltpu.CompilerParams(vmem_limit_bytes=GRANT)
    line_bytes = 4 * cells * lines
    source, fields, register = far(source), far(fields), far(register)
    metric_row, curvature_row = far(metric_row), far(curvature_row)
    semaphores = pltpu.SemaphoreType.DMA
    one_row = fast(1, cells)

    totals = pl.pallas_call(
        totals_kernel,
        in_specs=[hbm, hbm],
        out_specs=vmem,
        out_shape=fast(inner_count, groups, LANES),
        scratch_shapes=[fast(cells, lines), one_row, semaphores((3,))],
        compiler_params=params,
        cost_estimate=cost(line_bytes),
        name="totals",
    )(source, metric_row)
    inner_totals = lax.all_to_all(totals, near, 0, 0, axis_index_groups=turned(INNER_FIRST, inner_count))

    lower = np.tril(np.ones((cells, cells))) - 0.5 * np.eye(cells)
    lower = jnp.asarray(np.concatenate([lower] * 3, axis=1), jnp.bfloat16)
    message_one, message_two, running, spread = pl.pallas_call(
        send_kernel,
        in_specs=[smem, hbm, hbm, hbm, hbm, hbm],
        out_specs=[vmem, vmem, vmem, vmem],
        out_shape=[fast(*message_shape(lines)), fast(*message_shape(lines)), fast(cells, lines), fast(cells, LANES)],
        scratch_shapes=[
            fast(3, cells, lines),
            fast(cells, lines),
            one_row,
            fast(cells, LANES),
            pltpu.VMEM((cells, 3 * cells), jnp.bfloat16),
            semaphores((3, 3)),
        ],
        compiler_params=params,
        cost_estimate=cost(4 * line_bytes),
        name="send",
    )(kind, fields, source, metric_row, far(jnp.asarray(send_weights)), far(lower))

    slab_sums = pl.pallas_call(
        slab_kernel,
        in_specs=[vmem, hbm, hbm],
        out_specs=vmem,
        out_shape=fast(slab_count, groups, LANES),
        compiler_params=params,
        name="slab",
    )(keep(inner_totals), message_one, message_two)
    slab_totals = lax.all_to_all(slab_sums, "slab", 0, 0, axis_index_groups=turned(SLAB_FIRST, slab_count))

    even_pairs = [(i, i ^ 1) for i in range(count)]
    odd_pairs = [(i, i + 1 if i % 2 else i - 1) for i in range(1, count - 1)]
    got_two = lax.ppermute(message_two, line, odd_pairs)
    got_one = lax.ppermute(message_one, line, even_pairs)

    velocity, offset, rate = pl.pallas_call(
        velocity_kernel,
        in_specs=[smem, smem, vmem, vmem, vmem, vmem],
        out_specs=[vmem, vmem, vmem],
        out_shape=[fast(cells, lines), fast(1, lines), fast(devices, LANES)],
        compiler_params=params,
        cost_estimate=cost(2 * line_bytes),
        name="velocity",
    )(inner, slab, keep(running), keep(spread), keep(inner_totals), keep(slab_totals))

    order = np.arange(devices).reshape([lax.axis_size(axis) for axis in same_core])
    order = [int(i) for i in np.roll(order, [-turn for turn in RATE_FIRST], axis=(0, 1, 2)).ravel()]
    rates = lax.all_to_all(rate, same_core, 0, 0, axis_index_groups=[order], tiled=True)

    tendency, velocity_out = pl.pallas_call(
        tendency_kernel,
        in_specs=[smem, hbm, hbm, vmem, vmem, vmem, vmem, vmem, hbm, hbm],
        out_specs=[vmem, hbm],
        out_shape=[fast(3, cells, lines), pltpu.HBM((cells, lines), jnp.float32)],
        scratch_shapes=[
            fast(3, cells, lines),
            fast(cells, lines),
            fast(3, cells, DEPTH),
            one_row,
            pltpu.VMEM((2 * cells, DEPTH), jnp.bfloat16),
            pltpu.VMEM((2 * cells, DEPTH), jnp.bfloat16),
            pltpu.VMEM((cells, DEPTH), jnp.bfloat16),
            semaphores((3, 3)),
        ],
        compiler_params=params,
        cost_estimate=cost(12 * line_bytes),
        name="tendency",
    )(
        kind, fields, source, keep(velocity), keep(offset), keep(spread), got_one, got_two, curvature_row,
        far(jnp.asarray(solve_tables)),
    )

    rates, tendency = lax.optimization_barrier((rates, tendency))
    more_rates = lax.ppermute(rates, "core", [(0, 1), (1, 0)])
    new_fields, new_register = pl.pallas_call(
        update_kernel,
        in_specs=[hbm, hbm, vmem, vmem, vmem],
        out_specs=[hbm, hbm],
        out_shape=[pltpu.HBM((3, cells, lines), jnp.float32)] * 2,
        scratch_shapes=[fast(3, cells, lines), fast(3, cells, lines), semaphores((4, 3))],
        compiler_params=params,
        cost_estimate=cost(12 * line_bytes),
        name="update",
    )(fields, register, keep(tendency), keep(rates), keep(more_rates))
    return (new_fields, new_register, velocity_out)


def solution(mesh):
    along, across = mesh.devices.shape
    inner = 1
    while inner * inner < along:
        inner *= 2
    shape = (along // inner, inner // 2, 2, across)
    split = Mesh(mesh.devices.reshape(shape), ("slab", "ring", "core", "gz"))
    line = ("slab", "ring", "core")
    placed = (P(None, line, "gz"), P(None, line, "gz"), P(line, "gz"), P(line), P(line))
    return jax.shard_map(
        local,
        mesh=split,
        in_specs=placed,
        out_specs=(P(None, line, "gz"), P(None, line, "gz"), P(line, "gz")),
        check_vma=False,
    )
```

```python
import functools

import jax
import jax.numpy as jnp
import numpy as np
from jax import lax
from jax.experimental import pallas as pl
from jax.experimental.pallas import tpu as pltpu
from jax.sharding import Mesh
from jax.sharding import PartitionSpec as P

ALPHA_ONE = 1.0 / 3.0
COEF_ONE = 14.0 / 9.0
WIDE_ONE = 1.0 / 9.0
ALPHA_TWO = 2.0 / 11.0
COEF_TWO = 12.0 / 11.0
WIDE_TWO = 3.0 / 11.0
VISCOSITY = 0.25
DIFFUSIVITY = 0.2
COURANT = 1.2
KEEP_FACTOR = -5.0 / 9.0
STEP_FACTOR = 15.0 / 16.0

LANES = 128
TILE = 256
SLAB_FIRST = 4
INNER_FIRST = 0
RATE_FIRST = (4, 1, 2)
STEPS = 4
GRANT = 24 * 1024 * 1024
MESSAGE = 11
DEPTH = 256


def inverse(alpha, length):
    matrix = np.eye(length) + alpha * (np.eye(length, k=1) + np.eye(length, k=-1))
    return np.linalg.inv(matrix)


@functools.cache
def operators(cells):
    length = 4 * cells
    near_up, near_down = np.eye(length, k=1), np.eye(length, k=-1)
    far_up, far_down = np.eye(length, k=2), np.eye(length, k=-2)
    first = COEF_ONE / 2.0 * (near_up - near_down) + WIDE_ONE / 4.0 * (far_up - far_down)
    second = COEF_TWO * (near_up - 2.0 * np.eye(length) + near_down) + WIDE_TWO / 4.0 * (
        far_up - 2.0 * np.eye(length) + far_down
    )
    slope = inverse(ALPHA_ONE, length) @ first
    bend = inverse(ALPHA_TWO, length) @ second
    integral = -(np.tril(np.ones((length, length))) - 0.5 * np.eye(length))
    constant = slope @ np.ones(length)
    return slope, bend, slope @ integral, constant


def from_left(matrix, block, cells):
    start = block * cells
    part = matrix[start : start + cells, start - cells : start]
    weights = part[1]
    factors = part[:, cells - 2] / part[1, cells - 2]
    corner = np.zeros(cells)
    corner[0] = part[0, cells - 1] - factors[0] * part[1, cells - 1]
    return factors, weights, corner


def from_right(matrix, block, cells):
    start = block * cells
    part = matrix[start : start + cells, start + cells : start + 2 * cells]
    weights = part[cells - 2]
    factors = part[:, 1] / part[cells - 2, 1]
    corner = np.zeros(cells)
    corner[cells - 1] = part[cells - 1, 0] - factors[cells - 1] * part[cells - 2, 0]
    return factors, weights, corner


@functools.cache
def tables(cells):
    slope, bend, drift, constant = operators(cells)
    kinds = (0, 2, 1, 3)
    send = np.zeros((4, cells, LANES))
    solve = np.zeros((4, 3, cells, DEPTH))
    for kind, block in enumerate(kinds):
        odd = kind >= 2
        start = block * cells
        own = slice(start, start + cells)
        rest = np.zeros(4 * cells)
        if block == 3:
            rest[own] = constant[own]
        local = drift + rest[:, None] * (np.arange(4 * cells) < start)[None, :]
        for which, matrix in enumerate((slope, bend, local)):
            base = np.zeros((cells, cells + 8))
            base[:, :cells] = matrix[own, own]
            left, right = (0, 4) if odd else (4, 0)
            slot = 1 if which == 1 else 0
            if block > 0:
                factors, _, corner = from_left(matrix, block, cells)
                base[:, cells + left + slot] = factors
                base[:, cells + left + 2] = corner
            if block < 3:
                factors, _, corner = from_right(matrix, block, cells)
                base[:, cells + right + slot] = factors
                base[:, cells + right + 2] = corner
            if which == 2:
                base[:, cells + 1] = -rest[own]
            for copy in range(3):
                solve[kind, which, :, copy * cells : (copy + 1) * cells] = base[:, :cells]
                solve[kind, which, :, 3 * cells + 8 * copy : 3 * cells + 8 * copy + 8] = base[:, cells:]
            to_right = to_left = np.zeros(cells)
            sent = (slope, bend, drift)[which]
            if block < 2:
                to_right = from_left(sent, block + 1, cells)[1]
            elif block == 2:
                to_right = from_left(sent, 2, cells)[1]
            if block > 0:
                to_left = from_right(sent, block - 1, cells)[1]
            pair = (to_left, to_right) if odd else (to_right, to_left)
            send[kind, :, which] = pair[0]
            send[kind, :, 3 + which] = pair[1]
    return send.astype(np.float32), solve.astype(np.float32)


def column(row):
    size = row.shape[1]
    rows = lax.broadcasted_iota(jnp.int32, (size, size), 0)
    columns = lax.broadcasted_iota(jnp.int32, (size, size), 1)
    spread = jnp.broadcast_to(row, (size, size))
    return jnp.sum(jnp.where(rows == columns, spread, 0.0), axis=1, keepdims=True)


def halves(value):
    high = value.astype(jnp.bfloat16)
    low = (value - high.astype(jnp.float32)).astype(jnp.bfloat16)
    return high, low


def pieces_of(lines, count=STEPS):
    width = lines // count
    return [slice(start, start + width) for start in range(0, lines, width)]


def message_shape(lines):
    return 8, lines + (MESSAGE - 8) * (lines // 8)


def put(message, row, part, value):
    width = value.shape[1]
    fold = width // 2
    if row < 8:
        message[row : row + 1, part * width : (part + 1) * width] = value
        return
    start = STEPS * width + (row - 8) * fold
    for half in range(2):
        line = 2 * part + half
        message[line : line + 1, start : start + fold] = value[:, half * fold : (half + 1) * fold]


def take(message, row, part, width):
    fold = width // 2
    if row < 8:
        return message[row : row + 1, part * width : (part + 1) * width]
    start = STEPS * width + (row - 8) * fold
    return jnp.concatenate(
        [message[2 * part + half : 2 * part + half + 1, start : start + fold] for half in range(2)], axis=1
    )


def totals_kernel(source, metric, totals, held, held_metric, sems):
    cells, lines = source.shape
    metric_copy = pltpu.make_async_copy(metric, held_metric, sems.at[2])
    metric_copy.start()
    rows = [slice(0, cells // 2), slice(cells // 2, cells)]
    copies = [pltpu.make_async_copy(source.at[r, :], held.at[r, :], sems.at[i]) for i, r in enumerate(rows)]
    for copy in copies:
        copy.start()
    metric_copy.wait()
    scale = 1.0 / column(held_metric[...])
    total = jnp.zeros((1, lines), jnp.float32)
    for copy, r in zip(copies, rows):
        copy.wait()
        total += jnp.sum(held[r, :] * scale[r], axis=0, keepdims=True)
    for peer in range(totals.shape[0]):
        for k in range(lines // LANES):
            totals[peer, k : k + 1, :] = total[:, k * LANES : (k + 1) * LANES]


def send_kernel(
    kind, fields, source, metric, weights, lower, message_one, message_two, running, spread,
    held, held_source, held_metric, held_weights, held_lower, sems,
):
    cells, lines = source.shape
    pieces = pieces_of(lines, STEPS // 2)
    metric_copy = pltpu.make_async_copy(metric, held_metric, sems.at[2, 0])
    metric_copy.start()
    weights_copy = pltpu.make_async_copy(weights.at[kind[0]], held_weights, sems.at[2, 1])
    weights_copy.start()
    lower_copy = pltpu.make_async_copy(lower, held_lower, sems.at[2, 2])
    lower_copy.start()
    copies = []
    for i, p in enumerate(pieces):
        pair = (
            pltpu.make_async_copy(source.at[:, p], held_source.at[:, p], sems.at[1, i]),
            pltpu.make_async_copy(fields.at[:, :, p], held.at[:, :, p], sems.at[0, i]),
        )
        for copy in pair:
            copy.start()
        copies.append(pair)
    odd = kind[0] >= 2
    metric_copy.wait()
    weights_copy.wait()
    lower_copy.wait()
    chosen = held_weights[...]
    stretch = column(held_metric[...])
    spread[...] = jnp.broadcast_to(stretch, spread.shape)
    scale = 1.0 / stretch
    for i, p in enumerate(pieces_of(lines)):
        if i % 2 == 0:
            for copy in copies[i // 2]:
                copy.wait()
        scaled = held_source[:, p] * scale
        high = scaled.astype(jnp.bfloat16)
        rest = scaled - high.astype(jnp.float32)
        middle = rest.astype(jnp.bfloat16)
        low = (rest - middle.astype(jnp.float32)).astype(jnp.bfloat16)
        running[:, p] = jnp.dot(
            held_lower[...], jnp.concatenate([high, middle, low], axis=0), preferred_element_type=jnp.float32
        )
        for k in range(4):
            value = held[k, :, p] if k < 3 else scaled
            first, last = value[:1], value[cells - 1 :]
            for message, begin in ((message_one, 0), (message_two, 3)):
                row = 3 * k
                for which in range(2) if k < 3 else (2,):
                    weight = chosen[:, begin + which : begin + which + 1]
                    put(message, row, i, jnp.sum(value * weight, axis=0, keepdims=True))
                    row += 1
                put(message, row, i, jnp.where(odd, first, last) if begin == 0 else jnp.where(odd, last, first))


def slab_kernel(inner, after_one, after_two, sums):
    del after_one, after_two
    total = inner[0]
    for peer in range(1, inner.shape[0]):
        total += inner[peer]
    for peer in range(sums.shape[0]):
        sums[peer] = total


def velocity_kernel(place, slab, running, spread, inner, outer, velocity, offset, rate):
    stretch = spread[...]
    squared = 4.0 * VISCOSITY * stretch * stretch
    before = jnp.zeros(inner.shape[1:], jnp.float32)
    for peer in range(inner.shape[0]):
        owner = (peer + INNER_FIRST) % inner.shape[0]
        before += jnp.where(owner < place[0], inner[peer], 0.0)
    for peer in range(outer.shape[0]):
        owner = (peer + SLAB_FIRST) % outer.shape[0]
        before += jnp.where(owner < slab[0], outer[peer], 0.0)
    top = jnp.zeros((1, LANES), jnp.float32)
    for k in range(before.shape[0]):
        here = slice(k * LANES, (k + 1) * LANES)
        shift = before[k : k + 1, :]
        offset[:, here] = shift
        value = -(running[:, here] + shift)
        velocity[:, here] = value
        top = jnp.maximum(top, jnp.max(jnp.abs(value) * stretch + squared, axis=0, keepdims=True))
    peak = jnp.max(top, axis=1, keepdims=True)
    rate[...] = jnp.broadcast_to(peak, rate.shape)


def tendency_kernel(
    kind, fields, source, velocity, offset, spread, message_one, message_two, curvature, table,
    tendency, velocity_out,
    held_fields, held_source, held_table, held_curvature, mixed, mixed_scalar, drift, sems,
):
    cells, lines = source.shape
    pieces = pieces_of(lines, STEPS // 2)
    table_copy = pltpu.make_async_copy(table.at[kind[0]], held_table, sems.at[2, 0])
    table_copy.start()
    curvature_copy = pltpu.make_async_copy(curvature, held_curvature, sems.at[2, 1])
    curvature_copy.start()
    copies = []
    for i, p in enumerate(pieces):
        group = (
            pltpu.make_async_copy(source.at[:, p], held_source.at[:, p], sems.at[0, i]),
            pltpu.make_async_copy(fields.at[:, :, p], held_fields.at[:, :, p], sems.at[1, i]),
        )
        for copy in group:
            copy.start()
        copies.append(group)
    out_copy = pltpu.make_async_copy(velocity, velocity_out, sems.at[2, 2])
    out_copy.start()

    stretch = spread[:, :1]
    table_copy.wait()
    curvature_copy.wait()
    curving = column(held_curvature[...])
    slope, bend = held_table[0], held_table[1]
    lane = lax.broadcasted_iota(jnp.int32, (cells, DEPTH), 1)
    is_low = ((lane >= 2 * cells) & (lane < 3 * cells)) | (lane >= 3 * cells + 16)

    def split(value):
        high, low = halves(value)
        return jnp.where(is_low, low.astype(jnp.float32), high.astype(jnp.float32)).astype(jnp.bfloat16)

    field_x = stretch * slope
    field_xx = stretch * stretch * bend + curving * slope
    mixed[:cells, :] = split(field_x)
    mixed[cells:, :] = split(VISCOSITY * field_xx)
    mixed_scalar[:cells, :] = mixed[:cells, :]
    mixed_scalar[cells:, :] = split(DIFFUSIVITY * field_xx)
    drift[...] = split(stretch * held_table[2])

    def stacked(value, tail):
        high, low = halves(value)
        tail_high = tail.astype(jnp.bfloat16).astype(jnp.float32)
        tail_low = tail - tail_high
        tails = jnp.concatenate(
            [tail_high, tail_low, tail_high, jnp.zeros((DEPTH - 3 * cells - 24, width), jnp.float32)], axis=0
        ).astype(jnp.bfloat16)
        return jnp.concatenate([high, low, high, tails], axis=0)

    width = lines // STEPS
    blank = jnp.zeros((1, width), jnp.float32)

    def tails(rows, part, second):
        found = [[blank if row is None else take(message, row, part, width) for row in rows] for message in (message_one, message_two)]
        return jnp.concatenate([found[0][0], found[0][1] if second is None else second, *found[0][2:], *found[1]], axis=0)

    for i, p in enumerate(pieces_of(lines)):
        if i % 2 == 0:
            copies[i // 2][0].wait()
        scaled = held_source[:, p] * (1.0 / stretch)
        tail = tails((9, None, 10, None), i, offset[:, p])
        velocity_x = jnp.dot(drift[...], stacked(scaled, tail), preferred_element_type=jnp.float32)
        speed = velocity[:, p]
        if i % 2 == 0:
            copies[i // 2][1].wait()
        for k in range(3):
            field = held_fields[k, :, p]
            tail = tails((3 * k, 3 * k + 1, 3 * k + 2, None), i, None)
            weights = mixed if k < 2 else mixed_scalar
            right = stacked(field, tail)
            for low in range(0, width, TILE):
                here = slice(low, low + TILE)
                both = jnp.dot(weights[...], right[:, here], preferred_element_type=jnp.float32)
                there = slice(p.start + low, p.start + low + TILE)
                tendency[k, :, there] = both[cells:] - (
                    speed[:, here] * both[:cells] + field[:, here] * velocity_x[:, here]
                )
    out_copy.wait()


def update_kernel(fields, register, tendency, rates, more_rates, new_fields, new_register, held_fields, held_register, sems):
    cells = tendency.shape[1]
    edges = [0, 3 * cells // 8, 3 * cells // 4, cells]
    pieces = [(slice(None), slice(low, high)) for low, high in zip(edges[:-1], edges[1:])]
    arrivals = []
    for i, p in enumerate(pieces):
        pair = (
            pltpu.make_async_copy(register.at[p], held_register.at[p], sems.at[0, i]),
            pltpu.make_async_copy(fields.at[p], held_fields.at[p], sems.at[1, i]),
        )
        for copy in pair:
            copy.start()
        arrivals.append(pair)
    highest = jnp.maximum(rates[...], more_rates[...])
    time_step = COURANT / jnp.max(jnp.max(highest, axis=0, keepdims=True), axis=1, keepdims=True)
    departures = []
    for i, p in enumerate(pieces):
        arrivals[i][0].wait()
        updated = KEEP_FACTOR * held_register[p] + time_step * tendency[p]
        held_register[p] = updated
        departures.append(pltpu.make_async_copy(held_register.at[p], new_register.at[p], sems.at[2, i]))
        departures[-1].start()
        arrivals[i][1].wait()
        held_fields[p] = held_fields[p] + STEP_FACTOR * updated
        departures.append(pltpu.make_async_copy(held_fields.at[p], new_fields.at[p], sems.at[3, i]))
        departures[-1].start()
    for copy in departures:
        copy.wait()


def turned(first, count):
    return [[(i + first) % count for i in range(count)]]


def local(fields, register, source, metric, curvature):
    cells, lines = source.shape
    groups = lines // LANES
    near, line, same_core = ("ring", "core"), ("slab", "ring", "core"), ("slab", "ring", "gz")
    inner_count, slab_count = lax.axis_size(near), lax.axis_size("slab")
    count = inner_count * slab_count
    devices = lax.axis_size(same_core)
    inner, slab = lax.axis_index(near), lax.axis_index("slab")
    position = slab * inner_count + inner
    kind = jnp.where(position == 0, 0, jnp.where(position == count - 1, 3, 1 + position % 2))
    kind, inner, slab = (jnp.reshape(value, (1,)).astype(jnp.int32) for value in (kind, inner, slab))
    send_weights, solve_tables = tables(cells)
    metric_row, curvature_row = metric[None, :], curvature[None, :]

    smem = pl.BlockSpec(memory_space=pltpu.SMEM)
    vmem = pl.BlockSpec(memory_space=pltpu.VMEM)
    hbm = pl.BlockSpec(memory_space=pl.ANY)

    def shape(*sizes):
        return jax.ShapeDtypeStruct(sizes, jnp.float32)

    def fast(*sizes):
        return pltpu.VMEM(sizes, jnp.float32)

    def keep(value):
        return pltpu.with_memory_space_constraint(value, pltpu.VMEM)

    def far(value):
        return pltpu.with_memory_space_constraint(value, pltpu.HBM)

    def cost(bytes_accessed, flops=0):
        return pl.CostEstimate(flops=flops, bytes_accessed=bytes_accessed, transcendentals=0)

    params = pltpu.CompilerParams(vmem_limit_bytes=GRANT)
    line_bytes = 4 * cells * lines
    source, fields, register = far(source), far(fields), far(register)
    metric_row, curvature_row = far(metric_row), far(curvature_row)
    semaphores = pltpu.SemaphoreType.DMA
    one_row = fast(1, cells)

    totals = pl.pallas_call(
        totals_kernel,
        in_specs=[hbm, hbm],
        out_specs=vmem,
        out_shape=fast(inner_count, groups, LANES),
        scratch_shapes=[fast(cells, lines), one_row, semaphores((3,))],
        compiler_params=params,
        cost_estimate=cost(line_bytes),
        name="totals",
    )(source, metric_row)
    inner_totals = lax.all_to_all(totals, near, 0, 0, axis_index_groups=turned(INNER_FIRST, inner_count))

    lower = np.tril(np.ones((cells, cells))) - 0.5 * np.eye(cells)
    lower = jnp.asarray(np.concatenate([lower] * 3, axis=1), jnp.bfloat16)
    message_one, message_two, running, spread = pl.pallas_call(
        send_kernel,
        in_specs=[smem, hbm, hbm, hbm, hbm, hbm],
        out_specs=[vmem, vmem, vmem, vmem],
        out_shape=[fast(*message_shape(lines)), fast(*message_shape(lines)), fast(cells, lines), fast(cells, LANES)],
        scratch_shapes=[
            fast(3, cells, lines),
            fast(cells, lines),
            one_row,
            fast(cells, LANES),
            pltpu.VMEM((cells, 3 * cells), jnp.bfloat16),
            semaphores((3, 3)),
        ],
        compiler_params=params,
        cost_estimate=cost(4 * line_bytes),
        name="send",
    )(kind, fields, source, metric_row, far(jnp.asarray(send_weights)), far(lower))

    slab_sums = pl.pallas_call(
        slab_kernel,
        in_specs=[vmem, hbm, hbm],
        out_specs=vmem,
        out_shape=fast(slab_count, groups, LANES),
        compiler_params=params,
        name="slab",
    )(keep(inner_totals), message_one, message_two)
    slab_totals = lax.all_to_all(slab_sums, "slab", 0, 0, axis_index_groups=turned(SLAB_FIRST, slab_count))

    even_pairs = [(i, i ^ 1) for i in range(count)]
    odd_pairs = [(i, i + 1 if i % 2 else i - 1) for i in range(1, count - 1)]
    got_two = lax.ppermute(message_two, line, odd_pairs)
    got_one = lax.ppermute(message_one, line, even_pairs)

    velocity, offset, rate = pl.pallas_call(
        velocity_kernel,
        in_specs=[smem, smem, vmem, vmem, vmem, vmem],
        out_specs=[vmem, vmem, vmem],
        out_shape=[fast(cells, lines), fast(1, lines), fast(devices, LANES)],
        compiler_params=params,
        cost_estimate=cost(2 * line_bytes),
        name="velocity",
    )(inner, slab, keep(running), keep(spread), keep(inner_totals), keep(slab_totals))

    order = np.arange(devices).reshape([lax.axis_size(axis) for axis in same_core])
    order = [int(i) for i in np.roll(order, [-turn for turn in RATE_FIRST], axis=(0, 1, 2)).ravel()]
    rates = lax.all_to_all(rate, same_core, 0, 0, axis_index_groups=[order], tiled=True)

    tendency, velocity_out = pl.pallas_call(
        tendency_kernel,
        in_specs=[smem, hbm, hbm, vmem, vmem, vmem, vmem, vmem, hbm, hbm],
        out_specs=[vmem, hbm],
        out_shape=[fast(3, cells, lines), pltpu.HBM((cells, lines), jnp.float32)],
        scratch_shapes=[
            fast(3, cells, lines),
            fast(cells, lines),
            fast(3, cells, DEPTH),
            one_row,
            pltpu.VMEM((2 * cells, DEPTH), jnp.bfloat16),
            pltpu.VMEM((2 * cells, DEPTH), jnp.bfloat16),
            pltpu.VMEM((cells, DEPTH), jnp.bfloat16),
            semaphores((3, 3)),
        ],
        compiler_params=params,
        cost_estimate=cost(12 * line_bytes),
        name="tendency",
    )(
        kind, fields, source, keep(velocity), keep(offset), keep(spread), got_one, got_two, curvature_row,
        far(jnp.asarray(solve_tables)),
    )

    rates, tendency = lax.optimization_barrier((rates, tendency))
    more_rates = lax.ppermute(rates, "core", [(0, 1), (1, 0)])
    new_fields, new_register = pl.pallas_call(
        update_kernel,
        in_specs=[hbm, hbm, vmem, vmem, vmem],
        out_specs=[hbm, hbm],
        out_shape=[pltpu.HBM((3, cells, lines), jnp.float32)] * 2,
        scratch_shapes=[fast(3, cells, lines), fast(3, cells, lines), semaphores((4, 3))],
        compiler_params=params,
        cost_estimate=cost(12 * line_bytes),
        name="update",
    )(fields, register, keep(tendency), keep(rates), keep(more_rates))
    return (new_fields, new_register, velocity_out)


def solution(mesh):
    along, across = mesh.devices.shape
    inner = 1
    while inner * inner < along:
        inner *= 2
    shape = (along // inner, inner // 2, 2, across)
    split = Mesh(mesh.devices.reshape(shape), ("slab", "ring", "core", "gz"))
    line = ("slab", "ring", "core")
    placed = (P(None, line, "gz"), P(None, line, "gz"), P(line, "gz"), P(line), P(line))
    return jax.shard_map(
        local,
        mesh=split,
        in_specs=placed,
        out_specs=(P(None, line, "gz"), P(None, line, "gz"), P(line, "gz")),
        check_vma=False,
    )
```
